32 devices in a mesh: dp: 4 (over y, x), expert: 8 (over z, core).
Axes of the slice: x: 2, y: 2, z: 4, core: 2. Of those that a mesh axis runs over, the one named last changes fastest.
Arguments:
- tokens: bfloat16 [73728, 512], P(('dp', 'expert')), may hold values from -6 to 6
- gain_one: float32 [512], replicated, may hold values from 0.1 to 1.9
- w_qkv: bfloat16 [512, 1536], replicated, may hold values from -0.25 to 0.25
- w_attn_out: bfloat16 [512, 512], replicated, may hold values from -1 to 1
- gain_two: float32 [512], replicated, may hold values from 0.1 to 1.9
- w_router: bfloat16 [512, 8], replicated, may hold values from -0.1875 to 0.1875
- w_first: bfloat16 [8, 512, 2048], P('expert'), may hold values from -0.25 to 0.25
- w_second: bfloat16 [8, 2048, 512], P('expert'), may hold values from -1 to 1
- expert_ids: int32 [73728, 2], P(('dp', 'expert')), may hold values from 0 to 7, all different within a row
- priority_ranks: int32 [32, 2304], P(('dp', 'expert')), may hold values from 0 to 2303, each once within a row
- cotangent: float32 [73728, 512], P(('dp', 'expert')), may hold values from -6 to 6
Outputs:
- block_out: bfloat16 [73728, 512], P(('dp', 'expert'))
- grad_tokens: float32 [73728, 512], P(('dp', 'expert'))
- grad_gain_one: float32 [512], replicated
- grad_w_qkv: float32 [512, 1536], replicated
- grad_w_attn_out: float32 [512, 512], replicated
- grad_gain_two: float32 [512], replicated
- grad_w_router: float32 [512, 8], replicated
- grad_w_first: float32 [8, 512, 2048], P('expert')
- grad_w_second: float32 [8, 2048, 512], P('expert')
The draws below stay inside these ranges and needn't reach their ends.
Inputs may be any that keep to these rules, and one draw needn't show every extreme that they name: `expert_ids`: each row names two different experts, and every expert is named somewhere. `priority_ranks`: each row is a permutation of 0 to 2303.
All inputs are finite; a program needn't handle non-finite values.
Results may differ from the reference program's by a relative error of at most 0.015.
Values may be sent and summed in bfloat16 or wider, within the bound.
No kernel may reach another device: no remote copies, remote signals or barrier semaphores. Data moves between devices by JAX's collectives and lax.ppermute only.
A program may use at most 256 MiB of HBM per device.

```python
import jax
import jax.numpy as jnp
from jax import lax

D = 512
HEADS = 8
HEAD_DIM = 64
FF = 2048
PATCHES = 144
IMG_DEV = 16
TOK_DEV = 2304
GROUPS = 32
TOKENS = 73728
EXPERTS = 8
CAP = 288


def level_of(rng, dims, cuts, low, high):
    def one(position, shards_of):
        draws = jax.random.uniform(jax.random.fold_in(jax.random.fold_in(rng, 6), position), (shards_of,), jnp.float32, low / len(cuts), high / len(cuts))
        return jnp.repeat(jnp.exp(draws), dims[position] // shards_of).reshape((-1,) + (1,) * (len(dims) - position - 1))

    factor_of = one(*cuts[0])
    for cut in cuts[1:]:
        factor_of = factor_of * one(*cut)
    return factor_of


def different_ones(own_key, rows, count, top, lift):
    order = jax.random.permutation(jax.random.fold_in(own_key, 1), count)
    pull = order
    for power in range(3):
        pull = pull * pull // count
    pull = pull * lift // count
    tickets = jax.random.randint(jax.random.fold_in(own_key, 2), (rows, count), 0, 4096) + pull
    fixed_rows = jax.random.permutation(jax.random.fold_in(own_key, 3), rows)[jnp.arange(count) % rows]
    tickets = jnp.where(jnp.arange(rows)[:, None] == fixed_rows[None, :], 1 << 14, tickets)
    merit = tickets * count + jnp.arange(count)
    return lax.top_k(merit.astype(jnp.int32), top)[1].astype(jnp.int32)


def gaussian(stream_key, extent, deviation, most, split=(), held_as=jnp.bfloat16):
    values = deviation * jax.random.normal(stream_key, extent, jnp.float32)
    if split:
        values = values * level_of(stream_key, extent, split, -0.22, 0.18)
    return jnp.clip(values, -most, most).astype(held_as)


def setup_inputs(seed: int = 0) -> dict:
    splits = jax.random.split(jax.random.key(seed), 12)
    return {
        "tokens": gaussian(splits[0], (TOKENS, D), 1.0, 6.0, ((0, 32),)),
        "gain_one": jnp.clip(1.0 + 0.18 * jax.random.normal(splits[1], (D,), jnp.float32), 0.1, 1.9),
        "w_qkv": gaussian(splits[2], (D, 3 * D), D ** -0.5, 0.25),
        "w_attn_out": gaussian(splits[3], (D, D), (D // 12) ** -0.5, 1.0),
        "gain_two": jnp.clip(1.0 + 0.18 * jax.random.normal(splits[4], (D,), jnp.float32), 0.1, 1.9),
        "w_router": gaussian(splits[5], (D, EXPERTS), (2 * D) ** -0.5, 0.1875),
        "w_first": gaussian(splits[6], (EXPERTS, D, FF), D ** -0.5, 0.25, ((0, 8),)),
        "w_second": gaussian(splits[7], (EXPERTS, FF, D), (max(1, FF // (EXPERTS * EXPERTS))) ** -0.5, 1.0, ((0, 8),)),
        "expert_ids": different_ones(splits[8], TOKENS, EXPERTS, 2, 2048),
        "priority_ranks": jax.vmap(lambda own: jax.random.permutation(own, TOK_DEV))(jax.random.split(splits[9], GROUPS)).reshape((GROUPS, TOK_DEV)).astype(jnp.int32),
        "cotangent": gaussian(splits[10], (TOKENS, D), 1.0, 6.0, ((0, 32),), jnp.float32),
    }


@jax.custom_vjp
def low(v):
    return lax.optimization_barrier(v.astype(jnp.bfloat16)).astype(jnp.float32)

@jax.custom_vjp
def low_back(v):
    return v

def low_keep(v):
    return (low(v), None)

def low_pass(kept, grad):
    return (grad,)

def back_keep(v):
    return (v, None)

def back_low(kept, grad):
    return (low(grad),)
low.defvjp(low_keep, low_pass)
low_back.defvjp(back_keep, back_low)
HIGHEST = lax.Precision.HIGHEST
EPSILON = 1e-06

def layer_norm(values, gain):
    average = lax.optimization_barrier(jnp.mean(values, axis=-1, keepdims=True))
    centred = values - average
    variance = lax.optimization_barrier(jnp.mean(centred * centred, axis=-1, keepdims=True))
    return centred * lax.rsqrt(variance + EPSILON) * gain

def group_slots(group_args):
    ids, ranks = group_args
    catalog = jnp.arange(EXPERTS, dtype=jnp.int32)
    first_hot = (ids[:, 0:1] == catalog).astype(jnp.int32)
    second_hot = (ids[:, 1:2] == catalog).astype(jnp.int32)
    both_hot = jnp.concatenate([first_hot, second_hot], axis=1)
    ordered = jnp.zeros_like(both_hot).at[ranks.astype(jnp.int32)].set(both_hot)
    before = jnp.cumsum(ordered, axis=0) - ordered
    counted = before[ranks.astype(jnp.int32)]
    first_total = lax.optimization_barrier(jnp.sum(first_hot, axis=0))
    slot_first = lax.optimization_barrier(jnp.sum(counted[:, :EXPERTS] * first_hot, axis=1))
    slot_second = lax.optimization_barrier(jnp.sum((counted[:, EXPERTS:] + first_total) * second_hot, axis=1))
    return jnp.stack([slot_first, slot_second], axis=1).astype(jnp.int32)

def routing(expert_ids, priority_ranks):
    slots = lax.map(group_slots, (expert_ids.reshape(GROUPS, TOK_DEV, 2), priority_ranks)).reshape(TOKENS, 2)
    kept = slots < CAP
    group_of = (jnp.arange(TOKENS, dtype=jnp.int32) // TOK_DEV)[:, None]
    target = (group_of * EXPERTS + expert_ids) * CAP + slots
    target = jnp.where(kept, target, GROUPS * EXPERTS * CAP).astype(jnp.int32)
    return (target, kept.astype(jnp.float32))

def attention_group(rows, gain_one, w_qkv, w_attn_out):
    normed = low(layer_norm(rows, gain_one))
    packed = low(low_back(jnp.dot(normed, w_qkv, precision=HIGHEST)))
    grouped = packed.reshape(IMG_DEV, PATCHES, 3, HEADS, HEAD_DIM)
    queries = grouped[:, :, 0]
    keys = grouped[:, :, 1]
    values = grouped[:, :, 2]
    scores = jnp.einsum('bqhd,bkhd->bhqk', queries, keys, precision=HIGHEST) * HEAD_DIM ** (-0.5)
    scores = low_back(scores)
    weights = jax.nn.softmax(scores, axis=-1)
    mixed = jnp.einsum('bhqk,bkhd->bqhd', low(weights), values, precision=HIGHEST)
    mixed = low(low_back(mixed.reshape(TOK_DEV, D)))
    return low_back(jnp.dot(mixed, w_attn_out, precision=HIGHEST))

def expert_apply(expert_args):
    buffer_rows, first_layer, second_layer = expert_args
    pre_act = low_back(jnp.dot(buffer_rows, first_layer, precision=HIGHEST))
    hidden = low(jax.nn.gelu(pre_act))
    return low(low_back(jnp.dot(hidden, second_layer, precision=HIGHEST)))

def forward(inputs, gain_one, w_qkv, w_attn_out, gain_two, w_router, w_first, w_second, expert_ids, target, kept):

    def attend(rows):
        return attention_group(rows, gain_one, w_qkv, w_attn_out)
    attended = lax.map(jax.checkpoint(attend), inputs.reshape(GROUPS, TOK_DEV, D)).reshape(TOKENS, D)
    resid = inputs + attended
    normed = low(layer_norm(resid, gain_two))
    router = jax.nn.softmax(jnp.dot(normed, w_router, precision=HIGHEST), axis=-1)
    gates = jnp.take_along_axis(router, expert_ids, axis=1) * kept
    slots_all = GROUPS * EXPERTS * CAP
    buffers = jax.ops.segment_sum(normed, target[:, 0], num_segments=slots_all + 1)
    buffers = buffers + jax.ops.segment_sum(normed, target[:, 1], num_segments=slots_all + 1)
    buffers = low_back(buffers[:slots_all])
    by_expert = buffers.reshape(GROUPS, EXPERTS, CAP, D).transpose(1, 0, 2, 3).reshape(EXPERTS, GROUPS * CAP, D)
    outputs = lax.map(jax.checkpoint(expert_apply), (by_expert, w_first, w_second))
    returned = outputs.reshape(EXPERTS, GROUPS, CAP, D).transpose(1, 0, 2, 3).reshape(slots_all, D)
    returned = jnp.concatenate([returned, jnp.zeros((1, D), jnp.float32)], axis=0)
    mixture = gates[:, 0:1] * returned[target[:, 0]] + gates[:, 1:2] * returned[target[:, 1]]
    return resid + mixture

def reference(tokens, gain_one, w_qkv, w_attn_out, gain_two, w_router, w_first, w_second, expert_ids, priority_ranks, cotangent):
    target, kept = routing(expert_ids, priority_ranks)

    def closed(inputs, gain_a, qkv_a, out_a, gain_b, router_a, first_a, second_a):
        return forward(inputs, gain_a, qkv_a, out_a, gain_b, router_a, first_a, second_a, expert_ids, target, kept)
    result, pullback = jax.vjp(closed, tokens.astype(jnp.float32), gain_one, w_qkv.astype(jnp.float32), w_attn_out.astype(jnp.float32), gain_two, w_router.astype(jnp.float32), w_first.astype(jnp.float32), w_second.astype(jnp.float32))
    grads = pullback(cotangent)
    return (result.astype(jnp.bfloat16), grads[0], grads[1], grads[2], grads[3], grads[4], grads[5], grads[6], grads[7])
```

```python
from functools import partial

import jax
import jax.numpy as jnp
from jax import lax
from jax.experimental import pallas as pl
from jax.experimental.pallas import tpu as pltpu
from jax.sharding import PartitionSpec as P

D = 512
HEADS = 8
HEAD_DIM = 64
PATCHES = 144
QUAD = 256
EPSILON = 1e-06
EXTRA = 16
LANES = 128
F32 = jnp.float32
BF16 = jnp.bfloat16
VMEM_LIMIT = 60 * 1024 * 1024


def nn(a, b):
    return lax.dot_general(a, b, (((1,), (0,)), ((), ())), preferred_element_type=F32)


def nt(a, b):
    return lax.dot_general(a, b, (((1,), (1,)), ((), ())), preferred_element_type=F32)


def tn(a, b):
    return lax.dot_general(a, b, (((0,), (0,)), ((), ())), preferred_element_type=F32)


def standardise(values):
    average = jnp.mean(values, axis=-1, keepdims=True)
    centred = values - average
    variance = jnp.mean(centred * centred, axis=-1, keepdims=True)
    inverse = lax.rsqrt(variance + EPSILON)
    return centred * inverse, inverse


def standardise_back(hat, inverse, gain, grad):
    scaled = grad * gain
    mean_one = jnp.mean(scaled, axis=-1, keepdims=True)
    mean_two = jnp.mean(scaled * hat, axis=-1, keepdims=True)
    return inverse * (scaled - mean_one - hat * mean_two)


def halves(values):
    high = values.astype(BF16)
    low = (values - high.astype(F32)).astype(BF16)
    return high, low


def params(**more):
    return pltpu.CompilerParams(vmem_limit_bytes=VMEM_LIMIT, **more)


def whole(shape):
    zeros = (0,) * len(shape)
    return pl.BlockSpec(shape, lambda *_: zeros)


def route_kernel(experts, capacity, stride, ids_ref, ranks_ref, out_ref, cols_ref):
    toks = ids_ref.shape[1]
    catalog = lax.broadcasted_iota(jnp.int32, (experts, toks), 0)
    first_hot = (ids_ref[0:1, :] == catalog).astype(F32)
    second_hot = (ids_ref[1:2, :] == catalog).astype(F32)
    both = jnp.concatenate([first_hot, second_hot], axis=0).astype(BF16)
    first_total = jnp.sum(first_hot, axis=1, keepdims=True)
    ranks = ranks_ref[...].astype(F32)
    rank_rows = jnp.broadcast_to(ranks, (8, toks))
    rank_cols = jnp.transpose(rank_rows)[:, 0:1]
    tile = 256
    for start in range(0, toks, tile):
        part = slice(start, start + tile)
        earlier = (rank_cols < ranks[:, part]).astype(F32).astype(BF16)
        counted = nn(both, earlier)
        slot_first = jnp.sum(counted[:experts] * first_hot[:, part], axis=0, keepdims=True)
        slot_second = jnp.sum(
            (counted[experts:] + first_total) * second_hot[:, part], axis=0, keepdims=True
        )
        for row, slot in ((0, slot_first), (1, slot_second)):
            slot = slot.astype(jnp.int32)
            flat = ids_ref[row : row + 1, part] * stride + slot
            out_ref[row : row + 1, part] = jnp.where(slot < capacity, flat, -1)
    out_ref[2:, :] = jnp.full((6, toks), -1, jnp.int32)
    cols_ref[...] = jnp.transpose(out_ref[...].astype(F32)).astype(jnp.int32)


def route(ids, ranks, experts, capacity, stride):
    toks = ranks.shape[1]
    return pl.pallas_call(
        partial(route_kernel, experts, capacity, stride),
        out_shape=(
            jax.ShapeDtypeStruct((8, toks), jnp.int32),
            jax.ShapeDtypeStruct((toks, 8), jnp.int32),
        ),
        in_specs=[whole((2, toks)), whole((1, toks))],
        out_specs=(whole((8, toks)), whole((toks, 8))),
        grid=(1,),
        compiler_params=params(),
        name="route",
        cost_estimate=pl.CostEstimate(
            flops=2 * toks * toks * 128, bytes_accessed=toks * 48, transcendentals=0
        ),
    )(ids, ranks)


def selector_rows(base, rows, flat_ref):
    toks = flat_ref.shape[1]
    slot = lax.broadcasted_iota(jnp.int32, (rows, toks), 0) + base
    hit = (slot == flat_ref[0:1, :]) | (slot == flat_ref[1:2, :])
    return jnp.where(hit, 1.0, 0.0).astype(BF16)


def dispatch_grad_kernel(stride, flat_ref, grad_ref, out_ref, low_ref):
    expert = pl.program_id(0)

    @pl.when(expert == 0)
    def _():
        low_ref[...] = grad_ref[...].astype(BF16)

    chosen = selector_rows(expert * stride, out_ref.shape[1], flat_ref)
    out_ref[0] = nn(chosen, low_ref[...]).astype(BF16)


def dispatch_grad(flat, grad, experts, rows, stride):
    toks = grad.shape[0]
    return pl.pallas_call(
        partial(dispatch_grad_kernel, stride),
        out_shape=jax.ShapeDtypeStruct((experts, rows, D), BF16),
        in_specs=[whole((8, toks)), whole((toks, D))],
        out_specs=pl.BlockSpec((1, rows, D), lambda e: (e, 0, 0)),
        grid=(experts,),
        scratch_shapes=[pltpu.VMEM((toks, D), BF16)],
        compiler_params=params(),
        name="dispatch_grad",
        cost_estimate=pl.CostEstimate(
            flops=2 * toks * experts * rows * D, bytes_accessed=toks * D * 6, transcendentals=0
        ),
    )(flat, grad)


def dispatch_kernel(stride, rows, flat_ref, low_ref, router_ref, out_ref, split_ref):
    expert = pl.program_id(0)
    experts = pl.num_programs(0)

    @pl.when(expert == 0)
    def _():
        router = router_ref[...]
        high, low = halves(router)
        split_ref[:, :LANES] = high
        split_ref[:, LANES:] = low

    chosen = selector_rows(expert * stride, rows, flat_ref)
    out_ref[0, :rows] = nn(chosen, low_ref[...]).astype(BF16)
    picked = nn(chosen, split_ref[...])
    lane = lax.broadcasted_iota(jnp.int32, (rows, LANES), 1)
    here = lane == expert
    high = jnp.sum(jnp.where(here, picked[:, :LANES], 0.0), axis=1, keepdims=True)
    low = jnp.sum(jnp.where(here, picked[:, LANES:], 0.0), axis=1, keepdims=True)
    wide = jnp.where(lane == 0, high, jnp.where(lane == 1, low, 0.0))
    out_ref[0, rows:] = rows_of(wide, rows)


def rows_of(wide, rows):
    flipped = jnp.transpose(wide)[:EXTRA]
    return jnp.concatenate([flipped, jnp.zeros((EXTRA, D - rows), F32)], axis=1).astype(BF16)


def columns_of(extra, rows):
    flipped = jnp.transpose(extra.astype(F32))
    return flipped[:rows, 0:1] + flipped[:rows, 1:2]


def dispatch(flat, low, router, experts, rows, stride):
    toks = low.shape[0]
    return pl.pallas_call(
        partial(dispatch_kernel, stride, rows),
        out_shape=jax.ShapeDtypeStruct((experts, stride, D), BF16),
        in_specs=[whole((8, toks)), whole((toks, D)), whole((toks, LANES))],
        out_specs=pl.BlockSpec((1, stride, D), lambda e: (e, 0, 0)),
        grid=(experts,),
        scratch_shapes=[pltpu.VMEM((toks, 2 * LANES), BF16)],
        compiler_params=params(),
        name="dispatch",
        cost_estimate=pl.CostEstimate(
            flops=2 * toks * experts * rows * (D + 256),
            bytes_accessed=toks * D * 6,
            transcendentals=0,
        ),
    )(flat, low, router)


def head_stack(values):
    lane = lax.broadcasted_iota(jnp.int32, values.shape, 1) // HEAD_DIM
    zero = jnp.zeros_like(values)
    return jnp.concatenate([jnp.where(lane == h, values, zero) for h in range(4)], axis=0)


def forward_kernel(
    experts,
    x_ref,
    gain_one_ref,
    qkv_ref,
    out_w_ref,
    gain_two_ref,
    router_w_ref,
    packed_ref,
    log_ref,
    mixed_ref,
    resid_ref,
    low_two_ref,
    router_ref,
):
    images = log_ref.shape[0]
    x = x_ref[...].astype(F32)
    hat, _ = standardise(x)
    low_one = (hat * gain_one_ref[...]).astype(BF16)
    packed_ref[...] = nn(low_one, qkv_ref[...]).astype(BF16)
    for image in range(images):
        rows = slice(image * PATCHES, (image + 1) * PATCHES)
        for quad in range(2):
            cols = slice(quad * QUAD, (quad + 1) * QUAD)
            queries = packed_ref[rows, quad * QUAD : quad * QUAD + QUAD] * HEAD_DIM ** (-0.5)
            keys = packed_ref[rows, D + quad * QUAD : D + quad * QUAD + QUAD]
            values = packed_ref[rows, 2 * D + quad * QUAD : 2 * D + quad * QUAD + QUAD]
            values_t = jnp.transpose(values)
            scores = nt(head_stack(keys), queries.astype(BF16))
            parts = []
            for h in range(4):
                own = scores[h * PATCHES : (h + 1) * PATCHES]
                top = jnp.max(own, axis=0, keepdims=True)
                weights = jnp.exp(own - top)
                total = jnp.sum(weights, axis=0, keepdims=True)
                log_ref[image, quad * 4 + h : quad * 4 + h + 1, :] = top + jnp.log(total)
                part = nn(values_t[h * HEAD_DIM : (h + 1) * HEAD_DIM], weights.astype(BF16))
                parts.append(part / total)
            mixed_t = jnp.concatenate(parts, axis=0)
            mixed_ref[rows, cols] = jnp.transpose(mixed_t).astype(BF16)
    resid = x + nn(mixed_ref[...], out_w_ref[...])
    resid_ref[...] = resid
    hat_two, _ = standardise(resid)
    low_two = (hat_two * gain_two_ref[...]).astype(BF16)
    low_two_ref[...] = low_two
    logits = nn(low_two, router_w_ref[...])
    lane = lax.broadcasted_iota(jnp.int32, logits.shape, 1)
    logits = jnp.where(lane < experts, logits, -1e30)
    raised = jnp.exp(logits - jnp.max(logits, axis=1, keepdims=True))
    router_ref[...] = raised / jnp.sum(raised, axis=1, keepdims=True)


def attention_forward(x, gain_one, qkv, out_w, gain_two, router_w, experts, block):
    toks = x.shape[0]
    rows = block * PATCHES
    images = toks // PATCHES

    def tile(width):
        return pl.BlockSpec((rows, width), lambda i: (i, 0))

    return pl.pallas_call(
        partial(forward_kernel, experts),
        out_shape=(
            jax.ShapeDtypeStruct((toks, 3 * D), BF16),
            jax.ShapeDtypeStruct((images, HEADS, PATCHES), F32),
            jax.ShapeDtypeStruct((toks, D), BF16),
            jax.ShapeDtypeStruct((toks, D), F32),
            jax.ShapeDtypeStruct((toks, D), BF16),
            jax.ShapeDtypeStruct((toks, LANES), F32),
        ),
        in_specs=[
            tile(D),
            whole((1, D)),
            whole((D, 3 * D)),
            whole((D, D)),
            whole((1, D)),
            whole((D, LANES)),
        ],
        out_specs=(
            tile(3 * D),
            pl.BlockSpec((block, HEADS, PATCHES), lambda i: (i, 0, 0)),
            tile(D),
            tile(D),
            tile(D),
            tile(LANES),
        ),
        grid=(images // block,),
        compiler_params=params(),
        name="attention_forward",
        cost_estimate=pl.CostEstimate(
            flops=40_000_000_000, bytes_accessed=toks * D * 20, transcendentals=toks * 1152
        ),
    )(x, gain_one, qkv, out_w, gain_two, router_w)


GELU_C = 0.7978845608028654
GELU_A = 0.044715


def gelu_pair(v):
    square = v * v
    inner = v * (GELU_C + (GELU_C * GELU_A) * square)
    curve = jnp.tanh(inner)
    half = 0.5 + 0.5 * curve
    slope = half + 0.5 * v * (1.0 - curve * curve) * (GELU_C + (3.0 * GELU_C * GELU_A) * square)
    return v * half, slope


def expert_kernel(
    rows,
    received_ref,
    grad_ref,
    first_ref,
    second_ref,
    out_ref,
    back_ref,
    hidden_ref,
    d_pre_ref,
    d_out_ref,
    low_ref,
):
    groups = received_ref.shape[0]
    hidden_cols = first_ref.shape[2]
    for g in range(groups):
        span = slice(g * rows, (g + 1) * rows)
        gate = columns_of(received_ref[g, rows:, :], rows)
        low_ref[span] = received_ref[g, :rows]
        d_out_ref[span] = (gate * grad_ref[g].astype(F32)).astype(BF16)
    chunk = 512
    out = None
    back = None
    for start in range(0, hidden_cols, chunk):
        part = slice(start, start + chunk)
        pre = nn(low_ref[...], first_ref[0, :, part])
        act, slope = gelu_pair(pre)
        act = act.astype(BF16)
        hidden_ref[:, part] = act
        piece = nn(act, second_ref[0, part, :])
        out = piece if out is None else out + piece
        d_hidden = nt(d_out_ref[...], second_ref[0, part, :])
        d_pre = (d_hidden * slope).astype(BF16)
        d_pre_ref[:, part] = d_pre
        piece = nt(d_pre, first_ref[0, :, part])
        back = piece if back is None else back + piece
    lane = lax.broadcasted_iota(jnp.int32, (rows, LANES), 1)
    for g in range(groups):
        span = slice(g * rows, (g + 1) * rows)
        given = out[span].astype(BF16)
        out_ref[g, :rows] = given
        out_ref[g, rows:] = jnp.zeros((EXTRA, D), BF16)
        d_gate = jnp.sum(given.astype(F32) * grad_ref[g].astype(F32), axis=1, keepdims=True)
        high = d_gate.astype(BF16).astype(F32)
        wide = jnp.where(lane == 0, high, jnp.where(lane == 1, d_gate - high, 0.0))
        back_ref[g, :rows] = back[span].astype(BF16)
        back_ref[g, rows:] = rows_of(wide, rows)


def expert_apply(received, grad, first, second, block):
    groups, stride, _ = received.shape
    rows = grad.shape[1]
    wide = first.shape[2]
    total = groups * rows

    def flat(width):
        return pl.BlockSpec((block * rows, width), lambda i: (i, 0))

    return pl.pallas_call(
        partial(expert_kernel, rows),
        out_shape=(
            jax.ShapeDtypeStruct((groups, stride, D), BF16),
            jax.ShapeDtypeStruct((groups, stride, D), BF16),
            jax.ShapeDtypeStruct((total, wide), BF16),
            jax.ShapeDtypeStruct((total, wide), BF16),
            jax.ShapeDtypeStruct((total, D), BF16),
            jax.ShapeDtypeStruct((total, D), BF16),
        ),
        in_specs=[
            pl.BlockSpec((block, stride, D), lambda i: (i, 0, 0)),
            pl.BlockSpec((block, rows, D), lambda i: (i, 0, 0)),
            whole((1, D, wide)),
            whole((1, wide, D)),
        ],
        out_specs=(
            pl.BlockSpec((block, stride, D), lambda i: (i, 0, 0)),
            pl.BlockSpec((block, stride, D), lambda i: (i, 0, 0)),
            flat(wide),
            flat(wide),
            flat(D),
            flat(D),
        ),
        grid=(groups // block,),
        compiler_params=params(),
        name="expert_apply",
        cost_estimate=pl.CostEstimate(
            flops=8 * total * D * wide,
            bytes_accessed=total * wide * 4 + total * D * 12,
            transcendentals=total * wide,
        ),
    )(received, grad, first, second)


def expert_grads_kernel(low_ref, d_out_ref, hidden_ref, d_pre_ref, first_ref, second_ref):
    first_ref[0] = tn(low_ref[...], d_pre_ref[...]).astype(BF16)
    second_ref[0] = tn(hidden_ref[...], d_out_ref[...]).astype(BF16)


def expert_grads(low, d_out, hidden, d_pre):
    total, wide = hidden.shape
    chunk = 256
    return pl.pallas_call(
        expert_grads_kernel,
        out_shape=(
            jax.ShapeDtypeStruct((1, D, wide), BF16),
            jax.ShapeDtypeStruct((1, wide, D), BF16),
        ),
        in_specs=[
            whole((total, D)),
            whole((total, D)),
            pl.BlockSpec((total, chunk), lambda i: (0, i)),
            pl.BlockSpec((total, chunk), lambda i: (0, i)),
        ],
        out_specs=(
            pl.BlockSpec((1, D, chunk), lambda i: (0, 0, i)),
            pl.BlockSpec((1, chunk, D), lambda i: (0, i, 0)),
        ),
        grid=(wide // chunk,),
        compiler_params=params(),
        name="expert_grads",
        cost_estimate=pl.CostEstimate(
            flops=4 * total * D * wide, bytes_accessed=total * wide * 4, transcendentals=0
        ),
    )(low, d_out, hidden, d_pre)


def selector_cols(first, second, slots):
    slot = lax.broadcasted_iota(jnp.int32, (first.shape[0], slots), 1)
    hit = (slot == first) | (slot == second)
    return jnp.where(hit, 1.0, 0.0).astype(BF16)


def backward_kernel(
    experts,
    capacity_rows,
    flat_ref,
    returned_ref,
    cot_ref,
    resid_ref,
    router_ref,
    low_two_ref,
    mixed_ref,
    packed_ref,
    log_ref,
    x_ref,
    gain_one_ref,
    gain_two_ref,
    router_w_ref,
    out_w_ref,
    d_resid_ref,
    d_packed_ref,
    qkv_grad_ref,
    out_grad_ref,
    router_grad_ref,
    gain_two_grad_ref,
    gate_ref,
):
    step = pl.program_id(0)
    stride = capacity_rows + EXTRA
    slots = experts * stride

    @pl.when(step == 0)
    def _():
        lane = lax.broadcasted_iota(jnp.int32, (capacity_rows, LANES), 1)
        for e in range(experts):
            base = e * stride
            column = columns_of(returned_ref[base + capacity_rows : base + stride, :], capacity_rows)
            high = column.astype(BF16).astype(F32)
            wide = jnp.where(
                lane == e, high, jnp.where(lane == experts + e, column - high, 0.0)
            )
            gate_ref[base : base + capacity_rows] = wide.astype(BF16)
            gate_ref[base + capacity_rows : base + stride] = jnp.zeros((EXTRA, LANES), BF16)
        qkv_grad_ref[...] = jnp.zeros_like(qkv_grad_ref)
        out_grad_ref[...] = jnp.zeros_like(out_grad_ref)
        router_grad_ref[...] = jnp.zeros_like(router_grad_ref)
        gain_two_grad_ref[...] = jnp.zeros_like(gain_two_grad_ref)

    first, second = flat_ref[:, 0:1], flat_ref[:, 1:2]
    chosen = selector_cols(first, second, slots)
    d_two = nn(chosen, returned_ref[...])
    d_router = nn(chosen, gate_ref[...])
    d_router = d_router + pltpu.roll(d_router, LANES - experts, 1)
    router = router_ref[...]
    d_logits = router * (d_router - jnp.sum(router * d_router, axis=1, keepdims=True))
    high, low = halves(d_logits)
    d_two = d_two + nt(high, router_w_ref[...]) + nt(low, router_w_ref[...])
    low_two = low_two_ref[...]
    router_grad_ref[...] += tn(high, low_two) + tn(low, low_two)
    hat_two, inverse_two = standardise(resid_ref[...])
    gain_two_grad_ref[...] += jnp.sum(d_two * hat_two, axis=0, keepdims=True)
    d_resid = cot_ref[...] + standardise_back(hat_two, inverse_two, gain_two_ref[...], d_two)
    d_resid_ref[...] = d_resid
    d_attn = d_resid.astype(BF16)
    out_grad_ref[...] += tn(mixed_ref[...], d_attn)
    d_mixed = nt(d_attn, out_w_ref[...]).astype(BF16)
    scale = HEAD_DIM ** (-0.5)
    images = log_ref.shape[0]
    for image in range(images):
        rows = slice(image * PATCHES, (image + 1) * PATCHES)
        for quad in range(2):
            at = quad * QUAD
            queries = packed_ref[rows, at : at + QUAD] * scale
            queries = queries.astype(BF16)
            keys = packed_ref[rows, D + at : D + at + QUAD]
            values = packed_ref[rows, 2 * D + at : 2 * D + at + QUAD]
            grads = d_mixed[rows, at : at + QUAD]
            scores = nt(head_stack(keys), queries)
            d_probs = nt(head_stack(values), grads)
            keys_t = jnp.transpose(keys)
            lane = lax.broadcasted_iota(jnp.int32, (PATCHES, QUAD), 1) // HEAD_DIM
            d_values = jnp.zeros((PATCHES, QUAD), F32)
            d_keys = jnp.zeros((PATCHES, QUAD), F32)
            parts = []
            for h in range(4):
                own = slice(h * PATCHES, (h + 1) * PATCHES)
                log_row = log_ref[image, quad * 4 + h : quad * 4 + h + 1, :]
                probs = jnp.exp(scores[own] - log_row)
                d_own = d_probs[own]
                inner = jnp.sum(probs * d_own, axis=0, keepdims=True)
                d_scores = (probs * (d_own - inner)).astype(BF16)
                d_values = jnp.where(lane == h, nn(probs.astype(BF16), grads), d_values)
                d_keys = jnp.where(lane == h, nn(d_scores, queries), d_keys)
                parts.append(nn(keys_t[h * HEAD_DIM : (h + 1) * HEAD_DIM], d_scores))
            d_queries = jnp.transpose(jnp.concatenate(parts, axis=0)) * scale
            d_packed_ref[rows, at : at + QUAD] = d_queries.astype(BF16)
            d_packed_ref[rows, D + at : D + at + QUAD] = d_keys.astype(BF16)
            d_packed_ref[rows, 2 * D + at : 2 * D + at + QUAD] = d_values.astype(BF16)
    hat_one, _ = standardise(x_ref[...].astype(F32))
    low_one = (hat_one * gain_one_ref[...]).astype(BF16)
    qkv_grad_ref[...] += tn(low_one, d_packed_ref[...])


def attention_backward(
    flat,
    returned,
    cot,
    resid,
    router,
    low_two,
    mixed,
    packed,
    logs,
    x,
    gain_one,
    gain_two,
    router_w,
    out_w,
    experts,
    capacity_rows,
    block,
):
    toks = x.shape[0]
    rows = block * PATCHES
    images = toks // PATCHES
    slots = returned.shape[0]

    def tile(width):
        return pl.BlockSpec((rows, width), lambda i: (i, 0))

    return pl.pallas_call(
        partial(backward_kernel, experts, capacity_rows),
        out_shape=(
            jax.ShapeDtypeStruct((toks, D), F32),
            jax.ShapeDtypeStruct((toks, 3 * D), BF16),
            jax.ShapeDtypeStruct((D, 3 * D), F32),
            jax.ShapeDtypeStruct((D, D), F32),
            jax.ShapeDtypeStruct((LANES, D), F32),
            jax.ShapeDtypeStruct((1, D), F32),
        ),
        in_specs=[
            tile(8),
            whole((slots, D)),
            tile(D),
            tile(D),
            tile(LANES),
            tile(D),
            tile(D),
            tile(3 * D),
            pl.BlockSpec((block, HEADS, PATCHES), lambda i: (i, 0, 0)),
            tile(D),
            whole((1, D)),
            whole((1, D)),
            whole((D, LANES)),
            whole((D, D)),
        ],
        out_specs=(
            tile(D),
            tile(3 * D),
            whole((D, 3 * D)),
            whole((D, D)),
            whole((LANES, D)),
            whole((1, D)),
        ),
        grid=(images // block,),
        scratch_shapes=[pltpu.VMEM((slots, LANES), BF16)],
        compiler_params=params(),
        name="attention_backward",
        cost_estimate=pl.CostEstimate(
            flops=60_000_000_000, bytes_accessed=toks * D * 20, transcendentals=toks * 1152
        ),
    )(
        flat,
        returned,
        cot,
        resid,
        router,
        low_two,
        mixed,
        packed,
        logs,
        x,
        gain_one,
        gain_two,
        router_w,
        out_w,
    )


def input_kernel(d_packed_ref, d_resid_ref, x_ref, gain_one_ref, qkv_ref, grad_ref, gain_grad_ref):
    @pl.when(pl.program_id(0) == 0)
    def _():
        gain_grad_ref[...] = jnp.zeros_like(gain_grad_ref)

    d_one = nt(d_packed_ref[...], qkv_ref[...])
    hat, inverse = standardise(x_ref[...].astype(F32))
    gain_grad_ref[...] += jnp.sum(d_one * hat, axis=0, keepdims=True)
    grad_ref[...] = d_resid_ref[...] + standardise_back(hat, inverse, gain_one_ref[...], d_one)


def input_backward(d_packed, d_resid, x, gain_one, qkv, block):
    toks = x.shape[0]
    rows = block * PATCHES

    def tile(width):
        return pl.BlockSpec((rows, width), lambda i: (i, 0))

    return pl.pallas_call(
        input_kernel,
        out_shape=(jax.ShapeDtypeStruct((toks, D), F32), jax.ShapeDtypeStruct((1, D), F32)),
        in_specs=[tile(3 * D), tile(D), tile(D), whole((1, D)), whole((D, 3 * D))],
        out_specs=(tile(D), whole((1, D))),
        grid=(toks // rows,),
        compiler_params=params(),
        name="input_backward",
        cost_estimate=pl.CostEstimate(
            flops=2 * toks * D * 3 * D, bytes_accessed=toks * D * 20, transcendentals=0
        ),
    )(d_packed, d_resid, x, gain_one, qkv)


def combine_kernel(experts, stride, flat_ref, outputs_ref, resid_ref, router_ref, block_ref):
    first, second = flat_ref[:, 0:1], flat_ref[:, 1:2]
    lane = lax.broadcasted_iota(jnp.int32, router_ref.shape, 1) * stride
    router = router_ref[...]

    def gate(flat):
        mine = (flat >= lane) & (flat < lane + stride)
        return jnp.sum(jnp.where(mine, router, 0.0), axis=1, keepdims=True)

    slot = lax.broadcasted_iota(jnp.int32, (first.shape[0], experts * stride), 1)
    weight = jnp.where(slot == first, gate(first), jnp.where(slot == second, gate(second), 0.0))
    block_ref[...] = (resid_ref[...] + nn(weight.astype(BF16), outputs_ref[...])).astype(BF16)


def combine(flat, outputs, resid, router, experts, stride, block):
    toks = resid.shape[0]
    rows = block * PATCHES

    def tile(width):
        return pl.BlockSpec((rows, width), lambda i: (i, 0))

    return pl.pallas_call(
        partial(combine_kernel, experts, stride),
        out_shape=jax.ShapeDtypeStruct((toks, D), BF16),
        in_specs=[
            tile(8),
            whole((experts * stride, D)),
            tile(D),
            tile(LANES),
        ],
        out_specs=tile(D),
        grid=(toks // rows,),
        compiler_params=params(),
        name="combine",
        cost_estimate=pl.CostEstimate(
            flops=2 * toks * experts * stride * D, bytes_accessed=toks * D * 8, transcendentals=0
        ),
    )(flat, outputs, resid, router)


def exchange(values):
    return lax.all_to_all(values, "expert", split_axis=0, concat_axis=0, tiled=True)


def shards(
    tokens,
    gain_one,
    w_qkv,
    w_attn_out,
    gain_two,
    w_router,
    w_first,
    w_second,
    expert_ids,
    priority_ranks,
    cotangent,
):
    tok_rows = tokens.shape[0]
    experts = w_router.shape[1]
    capacity = max(2, tok_rows // experts)
    capacity_rows = -(-capacity // 16) * 16
    stride = capacity_rows + EXTRA
    gain_one = gain_one.reshape(1, D)
    gain_two = gain_two.reshape(1, D)
    router_w = jnp.pad(w_router, ((0, 0), (0, LANES - experts)))

    flat, flat_cols = route(expert_ids.T, priority_ranks, experts, capacity, stride)
    grad_rows = exchange(dispatch_grad(flat, cotangent, experts, capacity_rows, stride))
    packed, logs, mixed, resid, low_two, router = attention_forward(
        tokens, gain_one, w_qkv, w_attn_out, gain_two, router_w, experts, 2
    )
    received = exchange(dispatch(flat, low_two, router, experts, capacity_rows, stride))
    outputs, back, hidden, d_pre, d_out, low = expert_apply(
        received, grad_rows, w_first, w_second, 2
    )
    returned = exchange(back).reshape(experts * stride, D)
    outputs = exchange(outputs).reshape(experts * stride, D)
    first_grad, second_grad = expert_grads(low, d_out, hidden, d_pre)
    first_grad = lax.psum(first_grad, "dp").astype(F32)
    second_grad = lax.psum(second_grad, "dp").astype(F32)
    d_resid, d_packed, qkv_grad, out_grad, router_grad, gain_two_grad = attention_backward(
        flat_cols,
        returned,
        cotangent,
        resid,
        router,
        low_two,
        mixed,
        packed,
        logs,
        tokens,
        gain_one,
        gain_two,
        router_w,
        w_attn_out,
        experts,
        capacity_rows,
        2,
    )
    grad_tokens, gain_one_grad = input_backward(d_packed, d_resid, tokens, gain_one, w_qkv, 4)
    block_out = combine(flat_cols, outputs, resid, router, experts, stride, 4)
    router_grad = router_grad[:experts].T
    summed = lax.psum(
        (qkv_grad, out_grad, router_grad, gain_one_grad, gain_two_grad), ("dp", "expert")
    )
    return (
        block_out,
        grad_tokens,
        summed[3].reshape(D),
        summed[0],
        summed[1],
        summed[4].reshape(D),
        summed[2],
        first_grad,
        second_grad,
    )


def solution(mesh):
    both = P(("dp", "expert"), None)
    expert = P("expert", None, None)
    in_specs = (both, P(), P(), P(), P(), P(), expert, expert, both, both, both)
    out_specs = (both, both, P(), P(), P(), P(), P(), expert, expert)
    return jax.shard_map(shards, mesh=mesh, in_specs=in_specs, out_specs=out_specs, check_vma=False)
```

```python
from functools import partial

import jax
import jax.numpy as jnp
from jax import lax
from jax.experimental import pallas as pl
from jax.experimental.pallas import tpu as pltpu
from jax.sharding import Mesh
from jax.sharding import PartitionSpec as P

D = 512
HEADS = 8
HEAD_DIM = 64
PATCHES = 144
QUAD = 256
EPSILON = 1e-06
EXTRA = 16
SMALL = 8
LANES = 128
F32 = jnp.float32
BF16 = jnp.bfloat16
VMEM_LIMIT = 60 * 1024 * 1024


def nn(a, b):
    return lax.dot_general(a, b, (((1,), (0,)), ((), ())), preferred_element_type=F32)


def nt(a, b):
    return lax.dot_general(a, b, (((1,), (1,)), ((), ())), preferred_element_type=F32)


def tn(a, b):
    return lax.dot_general(a, b, (((0,), (0,)), ((), ())), preferred_element_type=F32)


def standardise(values):
    average = jnp.mean(values, axis=-1, keepdims=True)
    centred = values - average
    variance = jnp.mean(centred * centred, axis=-1, keepdims=True)
    inverse = lax.rsqrt(variance + EPSILON)
    return centred * inverse, inverse


def standardise_back(hat, inverse, gain, grad):
    scaled = grad * gain
    mean_one = jnp.mean(scaled, axis=-1, keepdims=True)
    mean_two = jnp.mean(scaled * hat, axis=-1, keepdims=True)
    return inverse * (scaled - mean_one - hat * mean_two)


def halves(values):
    high = values.astype(BF16)
    low = (values - high.astype(F32)).astype(BF16)
    return high, low


def params(**more):
    return pltpu.CompilerParams(vmem_limit_bytes=VMEM_LIMIT, **more)


def whole(shape):
    zeros = (0,) * len(shape)
    return pl.BlockSpec(shape, lambda *_: zeros)


def route_kernel(experts, capacity, stride, ids_ref, ranks_ref, out_ref, cols_ref):
    toks = ids_ref.shape[1]
    catalog = lax.broadcasted_iota(jnp.int32, (experts, toks), 0)
    first_hot = (ids_ref[0:1, :] == catalog).astype(F32)
    second_hot = (ids_ref[1:2, :] == catalog).astype(F32)
    both = jnp.concatenate([first_hot, second_hot], axis=0).astype(BF16)
    first_total = jnp.sum(first_hot, axis=1, keepdims=True)
    ranks = ranks_ref[...].astype(F32)
    rank_rows = jnp.broadcast_to(ranks, (8, toks))
    rank_cols = jnp.transpose(rank_rows)[:, 0:1]
    tile = 256
    for start in range(0, toks, tile):
        part = slice(start, start + tile)
        earlier = (rank_cols < ranks[:, part]).astype(F32).astype(BF16)
        counted = nn(both, earlier)
        slot_first = jnp.sum(counted[:experts] * first_hot[:, part], axis=0, keepdims=True)
        slot_second = jnp.sum(
            (counted[experts:] + first_total) * second_hot[:, part], axis=0, keepdims=True
        )
        for row, slot in ((0, slot_first), (1, slot_second)):
            slot = slot.astype(jnp.int32)
            flat = ids_ref[row : row + 1, part] * stride + slot
            out_ref[row : row + 1, part] = jnp.where(slot < capacity, flat, -1)
    out_ref[2:, :] = jnp.full((6, toks), -1, jnp.int32)
    cols_ref[...] = jnp.transpose(out_ref[...].astype(F32)).astype(jnp.int32)


def route(ids, ranks, experts, capacity, stride):
    toks = ranks.shape[1]
    return pl.pallas_call(
        partial(route_kernel, experts, capacity, stride),
        out_shape=(
            jax.ShapeDtypeStruct((8, toks), jnp.int32),
            jax.ShapeDtypeStruct((toks, 8), jnp.int32),
        ),
        in_specs=[whole((2, toks)), whole((1, toks))],
        out_specs=(whole((8, toks)), whole((toks, 8))),
        grid=(1,),
        compiler_params=params(),
        name="route",
        cost_estimate=pl.CostEstimate(
            flops=2 * toks * toks * 128, bytes_accessed=toks * 48, transcendentals=0
        ),
    )(ids, ranks)


def selector_rows(base, rows, flat_ref):
    toks = flat_ref.shape[1]
    slot = lax.broadcasted_iota(jnp.int32, (rows, toks), 0) + base
    hit = (slot == flat_ref[0:1, :]) | (slot == flat_ref[1:2, :])
    return jnp.where(hit, 1.0, 0.0).astype(BF16)


def dispatch_grad_kernel(stride, mine_ref, flat_ref, grad_ref, out_ref, low_ref):
    step = pl.program_id(0)

    @pl.when(step == 0)
    def _():
        low_ref[...] = grad_ref[...].astype(BF16)

    chosen = selector_rows((step ^ mine_ref[0]) * stride, out_ref.shape[1], flat_ref)
    out_ref[0] = nn(chosen, low_ref[...]).astype(BF16)


def dispatch_grad(mine, flat, grad, experts, rows, stride):
    toks = grad.shape[0]
    return pl.pallas_call(
        partial(dispatch_grad_kernel, stride),
        out_shape=jax.ShapeDtypeStruct((experts, rows, D), BF16),
        in_specs=[pl.BlockSpec(memory_space=pltpu.SMEM), whole((8, toks)), whole((toks, D))],
        out_specs=pl.BlockSpec((1, rows, D), lambda e: (e, 0, 0)),
        grid=(experts,),
        scratch_shapes=[pltpu.VMEM((toks, D), BF16)],
        compiler_params=params(),
        name="dispatch_grad",
        cost_estimate=pl.CostEstimate(
            flops=4 * toks * experts * rows * D, bytes_accessed=toks * D * 6, transcendentals=0
        ),
    )(mine, flat, grad)


def dispatch_kernel(stride, steps, flat_ref, low_ref, *out_refs):
    for k, out_ref in zip(steps, out_refs):
        chosen = selector_rows(k * stride, out_ref.shape[0], flat_ref)
        out_ref[...] = nn(chosen, low_ref[...]).astype(BF16)


def dispatch(flat, low, steps, rows, stride):
    toks = low.shape[0]
    return pl.pallas_call(
        partial(dispatch_kernel, stride, steps),
        out_shape=(jax.ShapeDtypeStruct((rows, D), BF16),) * len(steps),
        in_specs=[whole((8, toks)), whole((toks, D))],
        out_specs=(whole((rows, D)),) * len(steps),
        grid=(1,),
        compiler_params=params(),
        name="dispatch",
        cost_estimate=pl.CostEstimate(
            flops=4 * toks * len(steps) * rows * D, bytes_accessed=toks * D * 4, transcendentals=0
        ),
    )(flat, low)


def rows_of(wide, rows):
    flipped = jnp.transpose(wide)[:EXTRA]
    return jnp.concatenate([flipped, jnp.zeros((EXTRA, D - rows), F32)], axis=1).astype(BF16)


def columns_of(extra, rows):
    flipped = jnp.transpose(extra.astype(F32))
    return flipped[:rows, 0:1] + flipped[:rows, 1:2]


def router_softmax(low, router_w, experts):
    logits = nn(low, router_w)
    lane = lax.broadcasted_iota(jnp.int32, logits.shape, 1)
    logits = jnp.where(lane < experts, logits, -1e30)
    raised = jnp.exp(logits - jnp.max(logits, axis=1, keepdims=True))
    return raised / jnp.sum(raised, axis=1, keepdims=True)


def head_stack(values):
    lane = lax.broadcasted_iota(jnp.int32, values.shape, 1) // HEAD_DIM
    zero = jnp.zeros_like(values)
    return jnp.concatenate([jnp.where(lane == h, values, zero) for h in range(4)], axis=0)


def forward_kernel(
    experts,
    x_ref,
    gain_one_ref,
    qkv_ref,
    out_w_ref,
    gain_two_ref,
    router_w_ref,
    packed_ref,
    log_ref,
    mixed_ref,
    resid_ref,
    low_two_ref,
    router_ref,
):
    images = log_ref.shape[0]
    x = x_ref[...].astype(F32)
    hat, _ = standardise(x)
    low_one = (hat * gain_one_ref[...]).astype(BF16)
    packed_ref[...] = nn(low_one, qkv_ref[...]).astype(BF16)
    for image in range(images):
        rows = slice(image * PATCHES, (image + 1) * PATCHES)
        for quad in range(2):
            cols = slice(quad * QUAD, (quad + 1) * QUAD)
            queries = packed_ref[rows, quad * QUAD : quad * QUAD + QUAD] * HEAD_DIM ** (-0.5)
            keys = packed_ref[rows, D + quad * QUAD : D + quad * QUAD + QUAD]
            values = packed_ref[rows, 2 * D + quad * QUAD : 2 * D + quad * QUAD + QUAD]
            values_t = jnp.transpose(values)
            scores = nt(head_stack(keys), queries.astype(BF16))
            parts = []
            for h in range(4):
                own = scores[h * PATCHES : (h + 1) * PATCHES]
                top = jnp.max(own, axis=0, keepdims=True)
                weights = jnp.exp(own - top)
                total = jnp.sum(weights, axis=0, keepdims=True)
                log_ref[image, quad * 4 + h : quad * 4 + h + 1, :] = top + jnp.log(total)
                part = nn(values_t[h * HEAD_DIM : (h + 1) * HEAD_DIM], weights.astype(BF16))
                parts.append(part / total)
            mixed_t = jnp.concatenate(parts, axis=0)
            mixed_ref[rows, cols] = jnp.transpose(mixed_t).astype(BF16)
    resid = x + nn(mixed_ref[...], out_w_ref[...])
    resid_ref[...] = resid
    hat_two, _ = standardise(resid)
    low_two = (hat_two * gain_two_ref[...]).astype(BF16)
    low_two_ref[...] = low_two
    router_ref[...] = router_softmax(low_two, router_w_ref[...], experts)


def attention_forward(x, gain_one, qkv, out_w, gain_two, router_w, experts, block):
    toks = x.shape[0]
    rows = block * PATCHES
    images = toks // PATCHES

    def tile(width):
        return pl.BlockSpec((rows, width), lambda i: (i, 0))

    return pl.pallas_call(
        partial(forward_kernel, experts),
        out_shape=(
            jax.ShapeDtypeStruct((toks, 3 * D), BF16),
            jax.ShapeDtypeStruct((images, HEADS, PATCHES), F32),
            jax.ShapeDtypeStruct((toks, D), BF16),
            jax.ShapeDtypeStruct((toks, D), F32),
            jax.ShapeDtypeStruct((toks, D), BF16),
            jax.ShapeDtypeStruct((toks, LANES), F32),
        ),
        in_specs=[
            tile(D),
            whole((1, D)),
            whole((D, 3 * D)),
            whole((D, D)),
            whole((1, D)),
            whole((D, LANES)),
        ],
        out_specs=(
            tile(3 * D),
            pl.BlockSpec((block, HEADS, PATCHES), lambda i: (i, 0, 0)),
            tile(D),
            tile(D),
            tile(D),
            tile(LANES),
        ),
        grid=(images // block,),
        compiler_params=params(),
        name="attention_forward",
        cost_estimate=pl.CostEstimate(
            flops=31_000_000_000, bytes_accessed=toks * D * 20, transcendentals=0
        ),
    )(x, gain_one, qkv, out_w, gain_two, router_w)


GELU_C = 0.7978845608028654
GELU_A = 0.044715


def gelu_pair(v):
    square = v * v
    inner = v * (GELU_C + (GELU_C * GELU_A) * square)
    curve = jnp.tanh(inner)
    half = 0.5 + 0.5 * curve
    slope = half + 0.5 * v * (1.0 - curve * curve) * (GELU_C + (3.0 * GELU_C * GELU_A) * square)
    return v * half, slope


def expert_kernel(experts, count, choices, sources_ref, lane_ref, pick_ref, *refs):
    received_refs = refs[:count]
    grad_ref, router_w_ref = refs[count : count + 2]
    first_choices = refs[count + 2 : count + 2 + choices]
    second_choices = refs[count + 2 + choices : count + 2 + 2 * choices]
    first_ref, second_ref, sem = refs[-3:]
    outs = refs[len(refs) - 3 - count - 5 : -3]
    back_refs = outs[:count]
    out_ref, hidden_ref, d_pre_ref, d_out_ref, low_ref = outs[count:]
    step = pl.program_id(0)

    @pl.when(step == 0)
    def _():
        for at, from_refs, to_ref in ((0, first_choices, first_ref), (1, second_choices, second_ref)):
            for n, from_ref in enumerate(from_refs):

                @pl.when(pick_ref[at] == n)
                def _():
                    pltpu.make_async_copy(from_ref, to_ref, sem.at[at]).start()

        pltpu.make_async_copy(first_choices[0], first_ref, sem.at[0]).wait()
        pltpu.make_async_copy(second_choices[0], second_ref, sem.at[1]).wait()

    rows = low_ref.shape[0]
    hidden_cols = first_ref.shape[2]
    for r in range(count):

        @pl.when(step == r)
        def _():
            low_ref[...] = received_refs[r][...]

    lane = lax.broadcasted_iota(jnp.int32, (rows, LANES), 1)
    router = router_softmax(low_ref[...], router_w_ref[...], experts)
    gate = jnp.sum(jnp.where(lane == lane_ref[0], router, 0.0), axis=1, keepdims=True)
    d_out_ref[...] = (gate * grad_ref[0].astype(F32)).astype(BF16)
    chunk = 512
    out = None
    back = None
    for start in range(0, hidden_cols, chunk):
        part = slice(start, start + chunk)
        pre = nn(low_ref[...], first_ref[0, :, part])
        act, slope = gelu_pair(pre)
        act = act.astype(BF16)
        hidden_ref[:, part] = act
        piece = nn(act, second_ref[0, part, :])
        out = piece if out is None else out + piece
        d_hidden = nt(d_out_ref[...], second_ref[0, part, :])
        d_pre = (d_hidden * slope).astype(BF16)
        d_pre_ref[:, part] = d_pre
        piece = nt(d_pre, first_ref[0, :, part])
        back = piece if back is None else back + piece
    given = out.astype(BF16)
    out_ref[0] = given
    d_gate = jnp.sum(given.astype(F32) * grad_ref[0].astype(F32), axis=1, keepdims=True)
    high = d_gate.astype(BF16).astype(F32)
    wide = jnp.where(lane == 0, high, jnp.where(lane == 1, d_gate - high, 0.0))
    extra = rows_of(wide, rows)
    back = back.astype(BF16)
    for r in range(count):

        @pl.when(step == r)
        def _():
            back_refs[r][:rows] = back
            back_refs[r][rows:] = extra


def expert_apply(at, sources, lane, received, grad, weights, router_w, experts, stride, kept):
    pick, first, second = weights
    groups, rows, _ = grad.shape
    wide = first[0].shape[2]
    total = groups * rows
    count = len(received)

    def flat(width):
        return pl.BlockSpec((rows, width), lambda j, *_: (at + j, 0))

    kept_shapes = (
        jax.ShapeDtypeStruct((groups, rows, D), BF16),
        jax.ShapeDtypeStruct((total, wide), BF16),
        jax.ShapeDtypeStruct((total, wide), BF16),
        jax.ShapeDtypeStruct((total, D), BF16),
        jax.ShapeDtypeStruct((total, D), BF16),
    )
    source = pl.BlockSpec((1, rows, D), lambda j, sources, *_: (sources[j], 0, 0))
    anywhere = pl.BlockSpec(memory_space=pl.ANY)
    given = count + 5 + 2 * len(first)
    results = pl.pallas_call(
        partial(expert_kernel, experts, count, len(first)),
        out_shape=(jax.ShapeDtypeStruct((stride, D), BF16),) * count + kept_shapes,
        grid_spec=pltpu.PrefetchScalarGridSpec(
            num_scalar_prefetch=3,
            in_specs=[whole((rows, D))] * count
            + [source, whole((D, LANES))]
            + [anywhere] * (2 * len(first) + len(kept)),
            out_specs=(whole((stride, D)),) * count
            + (source, flat(wide), flat(wide), flat(D), flat(D)),
            grid=(count,),
            scratch_shapes=[
                pltpu.VMEM((1, D, wide), BF16),
                pltpu.VMEM((1, wide, D), BF16),
                pltpu.SemaphoreType.DMA((2,)),
            ],
        ),
        input_output_aliases={given + n: count + n for n in range(len(kept))},
        compiler_params=params(),
        name="expert_apply",
        cost_estimate=pl.CostEstimate(
            flops=15 * count * rows * D * wide,
            bytes_accessed=count * rows * wide * 4,
            transcendentals=0,
        ),
    )(sources, lane, pick, *received, grad, router_w, *first, *second, *kept)
    return results[:count], results[count:]


def expert_grads_kernel(core_ref, low_ref, d_out_ref, hidden_ref, d_pre_ref, keep_ref, give_ref):
    first = tn(low_ref[...], d_pre_ref[...]).astype(BF16)
    second = tn(hidden_ref[...], d_out_ref[...]).astype(BF16)
    even = core_ref[0] == 0

    @pl.when(even)
    def _():
        keep_ref[0] = first
        give_ref[0] = second

    @pl.when(jnp.logical_not(even))
    def _():
        keep_ref[0] = second
        give_ref[0] = first


def expert_grads(core, low, d_out, hidden, d_pre):
    total, wide = hidden.shape
    block = pl.BlockSpec((1, D, D), lambda i: (i, 0, 0))
    return pl.pallas_call(
        expert_grads_kernel,
        out_shape=(jax.ShapeDtypeStruct((wide // D, D, D), BF16),) * 2,
        in_specs=[
            pl.BlockSpec(memory_space=pltpu.SMEM),
            whole((total, D)),
            whole((total, D)),
            pl.BlockSpec((total, D), lambda i: (0, i)),
            pl.BlockSpec((total, D), lambda i: (0, i)),
        ],
        out_specs=(block, block),
        grid=(wide // D,),
        compiler_params=params(),
        name="expert_grads",
        cost_estimate=pl.CostEstimate(
            flops=8 * total * D * wide, bytes_accessed=total * wide * 4, transcendentals=0
        ),
    )(core, low, d_out, hidden, d_pre)


def pair_kernel(picks_ref, keep_ref, got_ref, *out_refs):
    step = pl.program_id(0)
    total = (keep_ref[0].astype(F32) + got_ref[0].astype(F32)).astype(BF16)
    for r, out_ref in enumerate(out_refs):

        @pl.when(step == r)
        def _():
            out_ref[...] = total


def pair_quarters(picks, keep, got):
    quarter = pl.BlockSpec((1, D, D), lambda i, picks: (picks[i], 0, 0))
    return pl.pallas_call(
        pair_kernel,
        out_shape=(jax.ShapeDtypeStruct((D, D), BF16),) * 4,
        grid_spec=pltpu.PrefetchScalarGridSpec(
            num_scalar_prefetch=1,
            in_specs=[quarter, quarter],
            out_specs=(pl.BlockSpec((D, D), lambda i, picks: (0, 0)),) * 4,
            grid=(4,),
        ),
        compiler_params=params(),
        name="pair_quarters",
        cost_estimate=pl.CostEstimate(flops=D * D, bytes_accessed=D * D * 24, transcendentals=0),
    )(picks, keep, got)


def join_kernel(turn_ref, a_ref, b_ref, c_ref, d_ref, own_a_ref, own_c_ref, out_ref):
    def total(one_ref, two_ref, own_ref, flag):
        own = jnp.where(flag != 0, own_ref[...].astype(F32), 0.0)
        return (one_ref[...].astype(F32) + two_ref[...].astype(F32) + own).astype(BF16)

    left = total(a_ref, b_ref, own_a_ref, turn_ref[1])
    right = total(c_ref, d_ref, own_c_ref, turn_ref[2])
    straight = turn_ref[0] == 0

    @pl.when(straight)
    def _():
        out_ref[0] = left
        out_ref[1] = right

    @pl.when(jnp.logical_not(straight))
    def _():
        out_ref[0] = right
        out_ref[1] = left


def join_quarters(turn, pieces):
    return pl.pallas_call(
        join_kernel,
        out_shape=jax.ShapeDtypeStruct((2, D, D), BF16),
        in_specs=[pl.BlockSpec(memory_space=pltpu.SMEM)] + [whole((D, D))] * 6,
        out_specs=whole((2, D, D)),
        grid=(1,),
        compiler_params=params(),
        name="join_quarters",
        cost_estimate=pl.CostEstimate(flops=D * D, bytes_accessed=D * D * 12, transcendentals=0),
    )(turn, *pieces)


def unfold_kernel(corner_ref, *refs):
    first_ref, second_ref = refs[-2:]
    step = pl.program_id(0)
    for r in range(4):

        @pl.when(step == r)
        def _():
            first_ref[0] = refs[r][0].astype(F32)
            second_ref[0] = refs[r][1].astype(F32)


def unfold(corner, pieces):
    return pl.pallas_call(
        unfold_kernel,
        out_shape=(
            jax.ShapeDtypeStruct((1, D, 4 * D), F32),
            jax.ShapeDtypeStruct((1, 4 * D, D), F32),
        ),
        grid_spec=pltpu.PrefetchScalarGridSpec(
            num_scalar_prefetch=1,
            in_specs=[pl.BlockSpec((2, D, D), lambda i, corner: (0, 0, 0))] * 4,
            out_specs=(
                pl.BlockSpec((1, D, D), lambda i, corner: (0, 0, i ^ corner[0])),
                pl.BlockSpec((1, D, D), lambda i, corner: (0, i ^ corner[0], 0)),
            ),
            grid=(4,),
        ),
        compiler_params=params(),
        name="unfold",
        cost_estimate=pl.CostEstimate(flops=D * D, bytes_accessed=D * D * 48, transcendentals=0),
    )(corner, *pieces)


def selector_cols(first, second, slots):
    slot = lax.broadcasted_iota(jnp.int32, (first.shape[0], slots), 1)
    hit = (slot == first) | (slot == second)
    return jnp.where(hit, 1.0, 0.0).astype(BF16)


def backward_kernel(experts, capacity_rows, *refs):
    backward_body(experts, capacity_rows, refs[:experts], *refs[experts:])


def backward_body(
    experts,
    capacity_rows,
    back_refs,
    flat_ref,
    cot_ref,
    resid_ref,
    router_ref,
    low_two_ref,
    mixed_ref,
    packed_ref,
    log_ref,
    x_ref,
    gain_one_ref,
    gain_two_ref,
    router_w_ref,
    out_w_ref,
    order_ref,
    d_resid_ref,
    d_packed_ref,
    partial_ref,
    returned_ref,
    gate_ref,
    qkv_grad_ref,
    out_grad_ref,
    router_grad_ref,
    gain_two_grad_ref,
):
    step = pl.program_id(0)
    stride = capacity_rows + EXTRA
    slots = experts * stride

    @pl.when(step == 0)
    def _():
        lane = lax.broadcasted_iota(jnp.int32, (capacity_rows, LANES), 1)
        for e in range(experts):
            base = e * stride
            returned_ref[base : base + stride] = back_refs[e][...]
            column = columns_of(back_refs[e][capacity_rows:, :], capacity_rows)
            high = column.astype(BF16).astype(F32)
            wide = jnp.where(
                lane == e, high, jnp.where(lane == experts + e, column - high, 0.0)
            )
            gate_ref[base : base + capacity_rows] = wide.astype(BF16)
            gate_ref[base + capacity_rows : base + stride] = jnp.zeros((EXTRA, LANES), BF16)
        qkv_grad_ref[...] = jnp.zeros_like(qkv_grad_ref)
        out_grad_ref[...] = jnp.zeros_like(out_grad_ref)
        router_grad_ref[...] = jnp.zeros_like(router_grad_ref)
        gain_two_grad_ref[...] = jnp.zeros_like(gain_two_grad_ref)

    first, second = flat_ref[:, 0:1], flat_ref[:, 1:2]
    chosen = selector_cols(first, second, slots)
    d_two = nn(chosen, returned_ref[...])
    d_router = nn(chosen, gate_ref[...])
    d_router = d_router + pltpu.roll(d_router, LANES - experts, 1)
    router = router_ref[...]
    d_logits = router * (d_router - jnp.sum(router * d_router, axis=1, keepdims=True))
    high, low = halves(d_logits)
    d_two = d_two + nt(high, router_w_ref[...]) + nt(low, router_w_ref[...])
    low_two = low_two_ref[...]
    router_grad_ref[...] += tn(high, low_two) + tn(low, low_two)
    hat_two, inverse_two = standardise(resid_ref[...])
    gain_two_grad_ref[...] += jnp.sum(d_two * hat_two, axis=0, keepdims=True)
    d_resid = cot_ref[...] + standardise_back(hat_two, inverse_two, gain_two_ref[...], d_two)
    d_resid_ref[...] = d_resid
    d_attn = d_resid.astype(BF16)
    out_grad_ref[...] += tn(mixed_ref[...], d_attn)
    d_mixed = nt(d_attn, out_w_ref[...]).astype(BF16)
    scale = HEAD_DIM ** (-0.5)
    images = log_ref.shape[0]
    for image in range(images):
        rows = slice(image * PATCHES, (image + 1) * PATCHES)
        for quad in range(2):
            at = quad * QUAD
            queries = packed_ref[rows, at : at + QUAD] * scale
            queries = queries.astype(BF16)
            keys = packed_ref[rows, D + at : D + at + QUAD]
            values = packed_ref[rows, 2 * D + at : 2 * D + at + QUAD]
            grads = d_mixed[rows, at : at + QUAD]
            scores = nt(head_stack(keys), queries)
            d_probs = nt(head_stack(values), grads)
            keys_t = jnp.transpose(keys)
            lane = lax.broadcasted_iota(jnp.int32, (PATCHES, QUAD), 1) // HEAD_DIM
            d_values = jnp.zeros((PATCHES, QUAD), F32)
            d_keys = jnp.zeros((PATCHES, QUAD), F32)
            parts = []
            for h in range(4):
                own = slice(h * PATCHES, (h + 1) * PATCHES)
                log_row = log_ref[image, quad * 4 + h : quad * 4 + h + 1, :]
                probs = jnp.exp(scores[own] - log_row)
                d_own = d_probs[own]
                inner = jnp.sum(probs * d_own, axis=0, keepdims=True)
                d_scores = (probs * (d_own - inner)).astype(BF16)
                d_values = jnp.where(lane == h, nn(probs.astype(BF16), grads), d_values)
                d_keys = jnp.where(lane == h, nn(d_scores, queries), d_keys)
                parts.append(nn(keys_t[h * HEAD_DIM : (h + 1) * HEAD_DIM], d_scores))
            d_queries = jnp.transpose(jnp.concatenate(parts, axis=0)) * scale
            d_packed_ref[rows, at : at + QUAD] = d_queries.astype(BF16)
            d_packed_ref[rows, D + at : D + at + QUAD] = d_keys.astype(BF16)
            d_packed_ref[rows, 2 * D + at : 2 * D + at + QUAD] = d_values.astype(BF16)
    hat_one, _ = standardise(x_ref[...].astype(F32))
    low_one = (hat_one * gain_one_ref[...]).astype(BF16)
    qkv_grad_ref[...] += tn(low_one, d_packed_ref[...])

    @pl.when(step == pl.num_programs(0) - 1)
    def _():
        pieces, height, _ = partial_ref.shape
        piece = height - SMALL
        high, low = halves(router_grad_ref[...])
        router_grad = nn(order_ref[...], high) + nn(order_ref[...], low)
        small = jnp.concatenate(
            [router_grad[:experts], jnp.broadcast_to(gain_two_grad_ref[...], (SMALL, D))],
            axis=0,
        ).astype(BF16)
        for j in range(pieces):
            block, at = divmod(j * piece, D)
            if block < 3:
                rows = qkv_grad_ref[at : at + piece, block * D : (block + 1) * D]
            else:
                rows = out_grad_ref[at : at + piece, :]
            partial_ref[j, :piece] = rows.astype(BF16)
            if j * SMALL < experts + SMALL:
                partial_ref[j, piece:] = small[j * SMALL : (j + 1) * SMALL]
            else:
                partial_ref[j, piece:] = jnp.zeros((SMALL, D), BF16)


def attention_backward(
    returned,
    flat,
    cot,
    resid,
    router,
    low_two,
    mixed,
    packed,
    logs,
    x,
    gain_one,
    gain_two,
    router_w,
    out_w,
    order,
    experts,
    capacity_rows,
    pieces,
    block,
):
    toks = x.shape[0]
    height = 4 * D // pieces + SMALL
    rows = block * PATCHES
    images = toks // PATCHES
    stride = returned[0].shape[0]
    slots = experts * stride

    def tile(width):
        return pl.BlockSpec((rows, width), lambda i: (i, 0))

    return pl.pallas_call(
        partial(backward_kernel, experts, capacity_rows),
        out_shape=(
            jax.ShapeDtypeStruct((toks, D), F32),
            jax.ShapeDtypeStruct((toks, 3 * D), BF16),
            jax.ShapeDtypeStruct((pieces, height, D), BF16),
        ),
        in_specs=[whole((stride, D))] * experts
        + [
            tile(8),
            tile(D),
            tile(D),
            tile(LANES),
            tile(D),
            tile(D),
            tile(3 * D),
            pl.BlockSpec((block, HEADS, PATCHES), lambda i: (i, 0, 0)),
            tile(D),
            whole((1, D)),
            whole((1, D)),
            whole((D, LANES)),
            whole((D, D)),
            whole((LANES, LANES)),
        ],
        out_specs=(
            tile(D),
            tile(3 * D),
            whole((pieces, height, D)),
        ),
        grid=(images // block,),
        scratch_shapes=[
            pltpu.VMEM((slots, D), BF16),
            pltpu.VMEM((slots, LANES), BF16),
            pltpu.VMEM((D, 3 * D), F32),
            pltpu.VMEM((D, D), F32),
            pltpu.VMEM((LANES, D), F32),
            pltpu.VMEM((1, D), F32),
        ],
        compiler_params=params(),
        name="attention_backward",
        cost_estimate=pl.CostEstimate(
            flops=70_000_000_000, bytes_accessed=toks * D * 20, transcendentals=0
        ),
    )(
        *returned,
        flat,
        cot,
        resid,
        router,
        low_two,
        mixed,
        packed,
        logs,
        x,
        gain_one,
        gain_two,
        router_w,
        out_w,
        order,
    )


def input_kernel(d_packed_ref, d_resid_ref, x_ref, gain_one_ref, qkv_ref, grad_ref):
    d_one = nt(d_packed_ref[...], qkv_ref[...])
    hat, inverse = standardise(x_ref[...].astype(F32))
    grad_ref[...] = d_resid_ref[...] + standardise_back(hat, inverse, gain_one_ref[...], d_one)


def input_backward(d_packed, d_resid, x, gain_one, qkv, block):
    toks = x.shape[0]
    rows = block * PATCHES

    def tile(width):
        return pl.BlockSpec((rows, width), lambda i: (i, 0))

    return pl.pallas_call(
        input_kernel,
        out_shape=jax.ShapeDtypeStruct((toks, D), F32),
        in_specs=[tile(3 * D), tile(D), tile(D), whole((1, D)), whole((D, 3 * D))],
        out_specs=tile(D),
        grid=(toks // rows,),
        compiler_params=params(),
        name="input_backward",
        cost_estimate=pl.CostEstimate(
            flops=7 * toks * D * D * 3, bytes_accessed=toks * D * 10, transcendentals=0
        ),
    )(d_packed, d_resid, x, gain_one, qkv)


def combine_kernel(experts, rows, stride, mine_ref, flat_ref, outputs_ref, resid_ref, router_ref, block_ref):
    first, second = flat_ref[:, 0:1], flat_ref[:, 1:2]
    lane = lax.broadcasted_iota(jnp.int32, router_ref.shape, 1) * stride
    router = router_ref[...]

    def gate(flat):
        mine = (flat >= lane) & (flat < lane + stride)
        return jnp.sum(jnp.where(mine, router, 0.0), axis=1, keepdims=True)

    position = lax.broadcasted_iota(jnp.int32, (1, experts * rows), 1)
    owner = jnp.zeros_like(position)
    for e in range(1, experts):
        owner = owner + (position >= e * rows).astype(jnp.int32)
    slot = (owner ^ mine_ref[0]) * stride + (position - owner * rows)
    weight = jnp.where(slot == first, gate(first), jnp.where(slot == second, gate(second), 0.0))
    block_ref[...] = (resid_ref[...] + nn(weight.astype(BF16), outputs_ref[...])).astype(BF16)


def combine(mine, flat, outputs, resid, router, experts, stride, block):
    slots = outputs.shape[0]
    toks = resid.shape[0]
    rows = block * PATCHES

    def tile(width):
        return pl.BlockSpec((rows, width), lambda i: (i, 0))

    return pl.pallas_call(
        partial(combine_kernel, experts, slots // experts, stride),
        out_shape=jax.ShapeDtypeStruct((toks, D), BF16),
        in_specs=[
            pl.BlockSpec(memory_space=pltpu.SMEM),
            tile(8),
            whole((slots, D)),
            tile(D),
            tile(LANES),
        ],
        out_specs=tile(D),
        grid=(toks // rows,),
        compiler_params=params(),
        name="combine",
        cost_estimate=pl.CostEstimate(
            flops=5 * toks * experts * stride * D, bytes_accessed=toks * D * 8, transcendentals=0
        ),
    )(mine, flat, outputs, resid, router)


def finish_kernel(
    experts,
    core_ref,
    own_ref,
    other_ref,
    gain_one_ref,
    qkv_w_ref,
    qkv_ref,
    out_ref,
    router_ref,
    gain_two_ref,
    gain_one_grad_ref,
):
    count, height, _ = own_ref.shape
    piece = height - SMALL

    def spread(low_ref, high_ref):
        for j in range(2 * count):
            source = low_ref if j < count else high_ref
            rows = source[j % count, :piece].astype(F32)
            block, at = divmod(j * piece, D)
            if block < 3:
                qkv_ref[at : at + piece, block * D : (block + 1) * D] = rows
            else:
                out_ref[at : at + piece, :] = rows
            at = j * SMALL
            if at < experts:
                router_ref[at : at + SMALL] = source[j % count, piece:].astype(F32)
            elif at == experts:
                gain_two_ref[...] = source[j % count, piece : piece + 1].astype(F32)

    @pl.when(core_ref[0] == 0)
    def _():
        spread(own_ref, other_ref)

    @pl.when(core_ref[0] != 0)
    def _():
        spread(other_ref, own_ref)

    column = jnp.sum(qkv_ref[...] * qkv_w_ref[...].astype(F32), axis=1, keepdims=True)
    row = jnp.transpose(jnp.broadcast_to(column, (D, LANES)))[0:1]
    gain_one_grad_ref[...] = row / gain_one_ref[...]


def finish(core, own, other, gain_one, qkv, experts):
    count, height, _ = own.shape
    shapes = ((D, 3 * D), (D, D), (experts, D), (1, D), (1, D))
    return pl.pallas_call(
        partial(finish_kernel, experts),
        out_shape=tuple(jax.ShapeDtypeStruct(shape, F32) for shape in shapes),
        in_specs=[
            pl.BlockSpec(memory_space=pltpu.SMEM),
            whole((count, height, D)),
            whole((count, height, D)),
            whole((1, D)),
            whole((D, 3 * D)),
        ],
        out_specs=tuple(whole(shape) for shape in shapes),
        grid=(1,),
        compiler_params=params(),
        name="finish",
        cost_estimate=pl.CostEstimate(flops=D * D * 8, bytes_accessed=D * D * 24, transcendentals=0),
    )(core, own, other, gain_one, qkv)


SWAP = ((0, 1), (1, 0))


def spread_out(values, axes):
    return lax.all_to_all(values, axes, split_axis=0, concat_axis=0, tiled=True)


def sum_everywhere(parts, sums, beside, plan):
    count = parts.shape[0] // 2
    core = lax.axis_index("core")
    low, high = parts[:count], parts[count:]
    keep = jnp.where(core == 0, low, high)
    give = jnp.where(core == 0, high, low)
    got = lax.ppermute(give, "core", SWAP)
    pair = (keep.astype(F32) + got.astype(F32)).astype(BF16)
    sums = plan.join_grads(sums)
    pair, sums = lax.optimization_barrier((pair, sums))
    sums = plan.share_grads(sums)
    spread = spread_out(pair, plan.chips)
    spread, sums, beside = lax.optimization_barrier((spread, sums, beside))
    total = jnp.sum(spread.astype(F32), axis=0, keepdims=True).astype(BF16)
    total = jnp.broadcast_to(total, pair.shape)
    own = spread_out(total, plan.chips)
    return own, lax.ppermute(own, "core", SWAP), sums, beside


class Straight:
    def __init__(self, mesh):
        dp, expert = mesh.devices.shape
        self.devices = dp * expert
        self.sends = self.works = [range(k, k + 4) for k in range(0, expert, 4)]
        self.mesh = Mesh(mesh.devices.reshape(dp, expert // 2, 2), ("dp", "chip", "core"))
        self.everyone = ("dp", "chip", "core")
        self.owners = ("chip", "core")
        self.chips = ("dp", "chip")

    def mine(self):
        return jnp.zeros((), jnp.int32)

    def lane(self):
        return lax.axis_index(("chip", "core"))

    def place(self, expert):
        return expert

    def exchange(self, values):
        return spread_out(values, ("chip", "core"))

    def scatter(self, pieces):
        moved = self.exchange(jnp.stack(pieces))
        return [moved[k] for k in range(len(pieces))]

    def weights(self, first, second):
        return first, second

    def pass_on(self, weights, after):
        return (jnp.zeros((2,), jnp.int32), [weights[0]], [weights[1]]), after

    def start_grads(self, first, second):
        first = first.transpose(1, 0, 2).reshape(1, D, -1)
        second = second.reshape(1, -1, D)
        return lax.psum(first, "dp"), lax.psum(second, "dp")

    def join_grads(self, sums):
        return sums

    def share_grads(self, sums):
        return sums

    def end_grads(self, sums):
        return sums[0].astype(F32), sums[1].astype(F32)

    def core(self):
        return jnp.zeros((1,), jnp.int32)


class Halves:
    def __init__(self, mesh):
        self.devices = 32
        self.sends = [(1, 2, 4, 7), (3, 5, 6, 0)]
        self.works = [(0, 1, 2, 4), (3, 5, 6, 7)]
        self.mesh = Mesh(mesh.devices.reshape(2, 2, 2, 2, 2), ("y", "x", "zh", "zl", "core"))
        self.everyone = ("y", "x", "zh", "zl", "core")
        self.owners = ("zh", "zl", "core")
        self.chips = ("y", "x", "zh", "zl")
        bits = (0, 1)
        self.all = [(y, x, h, l, c) for y in bits for x in bits for h in bits for l in bits for c in bits]

    def mine(self):
        return lax.axis_index(("y", "x", "zl"))

    def lane(self):
        return jnp.zeros((), jnp.int32)

    def place(self, expert):
        low = (expert >> 1) & 1
        y = ((expert >> 2) & 1) ^ lax.axis_index("zh") ^ low
        return (4 * y + 2 * (expert & 1) + low) ^ self.mine()

    def exchange(self, values):
        return spread_out(values, ("y", "x", "zl"))

    def scatter(self, pieces):
        return [
            lax.ppermute(piece, ("y", "x", "zl"), [(i, i ^ k) for i in range(8)]) if k else piece
            for k, piece in enumerate(pieces)
        ]

    def send(self, values, route):
        pairs = []
        for source in self.all:
            target = route(*source)
            if target is not None and target != source:
                pairs.append((self.all.index(source), self.all.index(target)))
        return lax.ppermute(values, self.everyone, pairs)

    def weights(self, first, second):
        def start(core):
            def route(y, x, h, l, c):
                if c != x:
                    return None
                return (y, x, h, l, 1 - x) if y == l else (y, x, 1 - h, l, core)

            return route

        first_in = self.send(first, start(0))
        second_in = self.send(second, start(1))
        return first, second, first_in, second_in

    def pass_on(self, weights, after):
        def passed(core):
            return lambda y, x, h, l, c: (y, x, h, l, 1 - c) if y != l and c == core else None

        first, second, first_in, second_in = weights
        (first_in, second_in), after = lax.optimization_barrier(((first_in, second_in), after))
        first_on = self.send(first_in, passed(0))
        second_on = self.send(second_in, passed(1))
        y, x, low, core = (lax.axis_index(name) for name in ("y", "x", "zl", "core"))
        near = (core ^ x) & 1
        pick = jnp.stack([jnp.where(y == low, near, 1 + core), jnp.where(y == low, near, 2 - core)])
        return (pick, [first, first_in, first_on], [second, second_in, second_on]), after

    def core(self):
        return lax.axis_index("core").reshape(1)

    def start_grads(self, keep, give):
        y, x, core = (lax.axis_index(name) for name in ("y", "x", "core"))
        got = lax.ppermute(give, "core", SWAP)
        rounds = [(ry, rx) for rx in (0, 1) for ry in (0, 1)]
        picks = jnp.stack([2 * (y ^ ry) + (x ^ rx ^ core) for ry, rx in rounds])
        quarters = pair_quarters(picks, keep, got)
        sent = [
            self.send(quarter, lambda y, x, h, l, c: (y ^ ry, x ^ rx ^ c, h ^ y ^ l, l, x))
            for quarter, (ry, rx) in zip(quarters, rounds)
        ]
        return sent + [quarters[0], quarters[2]]

    def join_grads(self, pieces):
        y, x, low, core = (lax.axis_index(name) for name in ("y", "x", "zl", "core"))
        home = (y == low) & (x == core)
        turn = jnp.stack(
            [x ^ core, (home & (core == 0)).astype(jnp.int32), (home & (core == 1)).astype(jnp.int32)]
        )
        return join_quarters(turn, pieces)

    def share_grads(self, mine):
        return [mine] + [
            lax.ppermute(mine, ("y", "x"), [(i, i ^ step) for i in range(4)]) for step in (1, 2, 3)
        ]

    def end_grads(self, pieces):
        y, x = lax.axis_index("y"), lax.axis_index("x")
        return unfold((2 * y + x).reshape(1), pieces)


def shards(
    plan,
    tokens,
    gain_one,
    w_qkv,
    w_attn_out,
    gain_two,
    w_router,
    w_first,
    w_second,
    expert_ids,
    priority_ranks,
    cotangent,
):
    tok_rows = tokens.shape[0]
    experts = w_router.shape[1]
    capacity = max(2, tok_rows // experts)
    capacity_rows = -(-capacity // 16) * 16
    stride = capacity_rows + EXTRA
    gain_one = gain_one.reshape(1, D)
    gain_two = gain_two.reshape(1, D)
    places = plan.place(jnp.arange(experts, dtype=jnp.int32))
    order = (places[:, None] == jnp.arange(LANES, dtype=jnp.int32)).astype(BF16)
    router_w = jnp.dot(w_router, order, preferred_element_type=F32).astype(BF16)
    order = jnp.pad(order, ((0, LANES - experts), (0, 0)))

    mine = plan.mine().reshape(1)
    lane = plan.lane().reshape(1)

    weights = plan.weights(w_first, w_second)
    flat, flat_cols = route(plan.place(expert_ids.T), priority_ranks, experts, capacity, stride)
    grad_rows = plan.exchange(dispatch_grad(mine, flat, cotangent, experts, capacity_rows, stride))
    packed, logs, mixed, resid, low_two, router = attention_forward(
        tokens, gain_one, w_qkv, w_attn_out, gain_two, router_w, experts, 4
    )
    pieces = [None] * experts
    for steps in plan.sends:
        for k, piece in zip(steps, dispatch(flat, low_two, steps, capacity_rows, stride)):
            pieces[k] = piece
    weights, pieces[0] = plan.pass_on(weights, pieces[0])
    received = plan.scatter(pieces)
    back = [None] * experts
    kept = ()
    at = 0
    for steps in plan.works:
        sources = jnp.asarray(steps, jnp.int32) ^ mine
        some, kept = expert_apply(
            at,
            sources,
            lane,
            [received[k] for k in steps],
            grad_rows,
            weights,
            router_w,
            experts,
            stride,
            kept,
        )
        at += len(steps)
        for k, piece in zip(steps, some):
            back[k] = piece
    outputs, hidden, d_pre, d_out, low = kept
    returned = plan.scatter(back)
    early = [returned[k] for k in plan.works[0]]
    low, early = lax.optimization_barrier((low, early))
    for k, piece in zip(plan.works[0], early):
        returned[k] = piece
    keep, give = expert_grads(plan.core(), low, d_out, hidden, d_pre)
    returned, keep, give, outputs = lax.optimization_barrier((returned, keep, give, outputs))
    outputs = plan.exchange(outputs)
    sums = plan.start_grads(keep, give)
    d_resid, d_packed, parts = attention_backward(
        returned,
        flat_cols,
        cotangent,
        resid,
        router,
        low_two,
        mixed,
        packed,
        logs,
        tokens,
        gain_one,
        gain_two,
        router_w,
        w_attn_out,
        order,
        experts,
        capacity_rows,
        plan.devices,
        4,
    )
    parts, d_packed, outputs, sums = lax.optimization_barrier((parts, d_packed, outputs, sums))
    grad_tokens = input_backward(d_packed, d_resid, tokens, gain_one, w_qkv, 4)
    outputs = outputs.reshape(experts * capacity_rows, D)
    block_out = combine(mine, flat_cols, outputs, resid, router, experts, stride, 4)
    own, other, sums, beside = sum_everywhere(parts, sums, (grad_tokens, block_out), plan)
    grad_tokens, block_out = beside
    first_grad, second_grad = plan.end_grads(sums)
    own, first_grad, second_grad = lax.optimization_barrier((own, first_grad, second_grad))
    core = lax.axis_index("core").reshape(1)
    qkv_grad, out_grad, router_grad, gain_two_grad, gain_one_grad = finish(
        core, own, other, gain_one, w_qkv, experts
    )
    return (
        block_out,
        grad_tokens,
        gain_one_grad.reshape(D),
        qkv_grad,
        out_grad,
        gain_two_grad.reshape(D),
        router_grad.T,
        first_grad,
        second_grad,
    )


def solution(mesh):
    plan = Halves(mesh) if mesh.devices.shape == (4, 8) else Straight(mesh)
    both = P(plan.everyone, None)
    one = P(plan.owners, None, None)
    in_specs = (both, P(), P(), P(), P(), P(), one, one, both, both, both)
    out_specs = (both, both, P(), P(), P(), P(), P(), one, one)
    return jax.shard_map(
        partial(shards, plan),
        mesh=plan.mesh,
        in_specs=in_specs,
        out_specs=out_specs,
        check_vma=False,
    )
```

```python
from functools import partial

import jax
import jax.numpy as jnp
from jax import lax
from jax.experimental import pallas as pl
from jax.experimental.pallas import tpu as pltpu
from jax.sharding import Mesh
from jax.sharding import PartitionSpec as P

D = 512
HEADS = 8
HEAD_DIM = 64
PATCHES = 144
QUAD = 256
EPSILON = 1e-06
EXTRA = 16
SMALL = 8
LANES = 128
F32 = jnp.float32
BF16 = jnp.bfloat16
VMEM_LIMIT = 60 * 1024 * 1024


def nn(a, b):
    return lax.dot_general(a, b, (((1,), (0,)), ((), ())), preferred_element_type=F32)


def nt(a, b):
    return lax.dot_general(a, b, (((1,), (1,)), ((), ())), preferred_element_type=F32)


def tn(a, b):
    return lax.dot_general(a, b, (((0,), (0,)), ((), ())), preferred_element_type=F32)


def standardise(values):
    average = jnp.mean(values, axis=-1, keepdims=True)
    centred = values - average
    variance = jnp.mean(centred * centred, axis=-1, keepdims=True)
    inverse = lax.rsqrt(variance + EPSILON)
    return centred * inverse, inverse


def standardise_back(hat, inverse, gain, grad):
    scaled = grad * gain
    mean_one = jnp.mean(scaled, axis=-1, keepdims=True)
    mean_two = jnp.mean(scaled * hat, axis=-1, keepdims=True)
    return inverse * (scaled - mean_one - hat * mean_two)


def halves(values):
    high = values.astype(BF16)
    low = (values - high.astype(F32)).astype(BF16)
    return high, low


def params(**more):
    return pltpu.CompilerParams(vmem_limit_bytes=VMEM_LIMIT, **more)


def whole(shape):
    zeros = (0,) * len(shape)
    return pl.BlockSpec(shape, lambda *_: zeros)


def route_kernel(experts, capacity, stride, ids_ref, ranks_ref, out_ref, cols_ref):
    toks = ids_ref.shape[1]
    catalog = lax.broadcasted_iota(jnp.int32, (experts, toks), 0)
    first_hot = (ids_ref[0:1, :] == catalog).astype(F32)
    second_hot = (ids_ref[1:2, :] == catalog).astype(F32)
    both = jnp.concatenate([first_hot, second_hot], axis=0).astype(BF16)
    first_total = jnp.sum(first_hot, axis=1, keepdims=True)
    ranks = ranks_ref[...].astype(F32)
    rank_rows = jnp.broadcast_to(ranks, (8, toks))
    rank_cols = jnp.transpose(rank_rows)[:, 0:1]
    tile = 256
    for start in range(0, toks, tile):
        part = slice(start, start + tile)
        earlier = (rank_cols < ranks[:, part]).astype(F32).astype(BF16)
        counted = nn(both, earlier)
        slot_first = jnp.sum(counted[:experts] * first_hot[:, part], axis=0, keepdims=True)
        slot_second = jnp.sum(
            (counted[experts:] + first_total) * second_hot[:, part], axis=0, keepdims=True
        )
        for row, slot in ((0, slot_first), (1, slot_second)):
            slot = slot.astype(jnp.int32)
            flat = ids_ref[row : row + 1, part] * stride + slot
            out_ref[row : row + 1, part] = jnp.where(slot < capacity, flat, -1)
    out_ref[2:, :] = jnp.full((6, toks), -1, jnp.int32)
    cols_ref[...] = jnp.transpose(out_ref[...].astype(F32)).astype(jnp.int32)


def route(ids, ranks, experts, capacity, stride):
    toks = ranks.shape[1]
    return pl.pallas_call(
        partial(route_kernel, experts, capacity, stride),
        out_shape=(
            jax.ShapeDtypeStruct((8, toks), jnp.int32),
            jax.ShapeDtypeStruct((toks, 8), jnp.int32),
        ),
        in_specs=[whole((2, toks)), whole((1, toks))],
        out_specs=(whole((8, toks)), whole((toks, 8))),
        grid=(1,),
        compiler_params=params(),
        name="route",
        cost_estimate=pl.CostEstimate(
            flops=2 * toks * toks * 128, bytes_accessed=toks * 48, transcendentals=0
        ),
    )(ids, ranks)


def selector_rows(base, rows, flat_ref):
    toks = flat_ref.shape[1]
    slot = lax.broadcasted_iota(jnp.int32, (rows, toks), 0) + base
    hit = (slot == flat_ref[0:1, :]) | (slot == flat_ref[1:2, :])
    return jnp.where(hit, 1.0, 0.0).astype(BF16)


def dispatch_grad_kernel(stride, mine_ref, flat_ref, grad_ref, out_ref, low_ref):
    step = pl.program_id(0)

    @pl.when(step == 0)
    def _():
        low_ref[...] = grad_ref[...].astype(BF16)

    chosen = selector_rows((step ^ mine_ref[0]) * stride, out_ref.shape[1], flat_ref)
    out_ref[0] = nn(chosen, low_ref[...]).astype(BF16)


def dispatch_grad(mine, flat, grad, experts, rows, stride):
    toks = grad.shape[0]
    return pl.pallas_call(
        partial(dispatch_grad_kernel, stride),
        out_shape=jax.ShapeDtypeStruct((experts, rows, D), BF16),
        in_specs=[pl.BlockSpec(memory_space=pltpu.SMEM), whole((8, toks)), whole((toks, D))],
        out_specs=pl.BlockSpec((1, rows, D), lambda e: (e, 0, 0)),
        grid=(experts,),
        scratch_shapes=[pltpu.VMEM((toks, D), BF16)],
        compiler_params=params(),
        name="dispatch_grad",
        cost_estimate=pl.CostEstimate(
            flops=4 * toks * experts * rows * D, bytes_accessed=toks * D * 6, transcendentals=0
        ),
    )(mine, flat, grad)


def dispatch_kernel(stride, steps, flat_ref, low_ref, *out_refs):
    for k, out_ref in zip(steps, out_refs):
        chosen = selector_rows(k * stride, out_ref.shape[0], flat_ref)
        out_ref[...] = nn(chosen, low_ref[...]).astype(BF16)


def dispatch(flat, low, steps, rows, stride):
    toks = low.shape[0]
    return pl.pallas_call(
        partial(dispatch_kernel, stride, steps),
        out_shape=(jax.ShapeDtypeStruct((rows, D), BF16),) * len(steps),
        in_specs=[whole((8, toks)), whole((toks, D))],
        out_specs=(whole((rows, D)),) * len(steps),
        grid=(1,),
        compiler_params=params(),
        name="dispatch",
        cost_estimate=pl.CostEstimate(
            flops=4 * toks * len(steps) * rows * D, bytes_accessed=toks * D * 4, transcendentals=0
        ),
    )(flat, low)


def rows_of(wide, rows):
    flipped = jnp.transpose(wide)[:EXTRA]
    return jnp.concatenate([flipped, jnp.zeros((EXTRA, D - rows), F32)], axis=1).astype(BF16)


def columns_of(extra, rows):
    flipped = jnp.transpose(extra.astype(F32))
    return flipped[:rows, 0:1] + flipped[:rows, 1:2]


def router_softmax(low, router_w, experts):
    logits = nn(low, router_w)
    lane = lax.broadcasted_iota(jnp.int32, logits.shape, 1)
    logits = jnp.where(lane < experts, logits, -1e30)
    raised = jnp.exp(logits - jnp.max(logits, axis=1, keepdims=True))
    return raised / jnp.sum(raised, axis=1, keepdims=True)


def head_stack(values):
    lane = lax.broadcasted_iota(jnp.int32, values.shape, 1) // HEAD_DIM
    zero = jnp.zeros_like(values)
    return jnp.concatenate([jnp.where(lane == h, values, zero) for h in range(4)], axis=0)


def forward_kernel(
    experts,
    x_ref,
    gain_one_ref,
    qkv_ref,
    out_w_ref,
    gain_two_ref,
    router_w_ref,
    packed_ref,
    log_ref,
    mixed_ref,
    resid_ref,
    low_two_ref,
    router_ref,
):
    images = log_ref.shape[0]
    x = x_ref[...].astype(F32)
    hat, _ = standardise(x)
    low_one = (hat * gain_one_ref[...]).astype(BF16)
    packed_ref[...] = nn(low_one, qkv_ref[...]).astype(BF16)
    for image in range(images):
        rows = slice(image * PATCHES, (image + 1) * PATCHES)
        for quad in range(2):
            cols = slice(quad * QUAD, (quad + 1) * QUAD)
            queries = packed_ref[rows, quad * QUAD : quad * QUAD + QUAD] * HEAD_DIM ** (-0.5)
            keys = packed_ref[rows, D + quad * QUAD : D + quad * QUAD + QUAD]
            values = packed_ref[rows, 2 * D + quad * QUAD : 2 * D + quad * QUAD + QUAD]
            values_t = jnp.transpose(values)
            scores = nt(head_stack(keys), queries.astype(BF16))
            parts = []
            for h in range(4):
                own = scores[h * PATCHES : (h + 1) * PATCHES]
                top = jnp.max(own, axis=0, keepdims=True)
                weights = jnp.exp(own - top)
                total = jnp.sum(weights, axis=0, keepdims=True)
                log_ref[image, quad * 4 + h : quad * 4 + h + 1, :] = top + jnp.log(total)
                part = nn(values_t[h * HEAD_DIM : (h + 1) * HEAD_DIM], weights.astype(BF16))
                parts.append(part / total)
            mixed_t = jnp.concatenate(parts, axis=0)
            mixed_ref[rows, cols] = jnp.transpose(mixed_t).astype(BF16)
    resid = x + nn(mixed_ref[...], out_w_ref[...])
    resid_ref[...] = resid
    hat_two, _ = standardise(resid)
    low_two = (hat_two * gain_two_ref[...]).astype(BF16)
    low_two_ref[...] = low_two
    router_ref[...] = router_softmax(low_two, router_w_ref[...], experts)


def attention_forward(x, gain_one, qkv, out_w, gain_two, router_w, experts, block):
    toks = x.shape[0]
    rows = block * PATCHES
    images = toks // PATCHES

    def tile(width):
        return pl.BlockSpec((rows, width), lambda i: (i, 0))

    return pl.pallas_call(
        partial(forward_kernel, experts),
        out_shape=(
            jax.ShapeDtypeStruct((toks, 3 * D), BF16),
            jax.ShapeDtypeStruct((images, HEADS, PATCHES), F32),
            jax.ShapeDtypeStruct((toks, D), BF16),
            jax.ShapeDtypeStruct((toks, D), F32),
            jax.ShapeDtypeStruct((toks, D), BF16),
            jax.ShapeDtypeStruct((toks, LANES), F32),
        ),
        in_specs=[
            tile(D),
            whole((1, D)),
            whole((D, 3 * D)),
            whole((D, D)),
            whole((1, D)),
            whole((D, LANES)),
        ],
        out_specs=(
            tile(3 * D),
            pl.BlockSpec((block, HEADS, PATCHES), lambda i: (i, 0, 0)),
            tile(D),
            tile(D),
            tile(D),
            tile(LANES),
        ),
        grid=(images // block,),
        compiler_params=params(),
        name="attention_forward",
        cost_estimate=pl.CostEstimate(
            flops=31_000_000_000, bytes_accessed=toks * D * 20, transcendentals=0
        ),
    )(x, gain_one, qkv, out_w, gain_two, router_w)


GELU_C = 0.7978845608028654
GELU_A = 0.044715


def gelu_pair(v):
    square = v * v
    inner = v * (GELU_C + (GELU_C * GELU_A) * square)
    curve = jnp.tanh(inner)
    half = 0.5 + 0.5 * curve
    slope = half + 0.5 * v * (1.0 - curve * curve) * (GELU_C + (3.0 * GELU_C * GELU_A) * square)
    return v * half, slope


def expert_kernel(experts, count, choices, sources_ref, lane_ref, pick_ref, *refs):
    received_refs = refs[:count]
    grad_ref, router_w_ref = refs[count : count + 2]
    first_choices = refs[count + 2 : count + 2 + choices]
    second_choices = refs[count + 2 + choices : count + 2 + 2 * choices]
    first_ref, second_ref, sem = refs[-3:]
    outs = refs[len(refs) - 3 - count - 5 : -3]
    back_refs = outs[:count]
    out_ref, hidden_ref, d_pre_ref, d_out_ref, low_ref = outs[count:]
    step = pl.program_id(0)

    @pl.when(step == 0)
    def _():
        for at, from_refs, to_ref in ((0, first_choices, first_ref), (1, second_choices, second_ref)):
            for n, from_ref in enumerate(from_refs):

                @pl.when(pick_ref[at] == n)
                def _():
                    pltpu.make_async_copy(from_ref, to_ref, sem.at[at]).start()

        pltpu.make_async_copy(first_choices[0], first_ref, sem.at[0]).wait()
        pltpu.make_async_copy(second_choices[0], second_ref, sem.at[1]).wait()

    rows = low_ref.shape[0]
    hidden_cols = first_ref.shape[2]
    for r in range(count):

        @pl.when(step == r)
        def _():
            low_ref[...] = received_refs[r][...]

    lane = lax.broadcasted_iota(jnp.int32, (rows, LANES), 1)
    router = router_softmax(low_ref[...], router_w_ref[...], experts)
    gate = jnp.sum(jnp.where(lane == lane_ref[0], router, 0.0), axis=1, keepdims=True)
    d_out_ref[...] = (gate * grad_ref[0].astype(F32)).astype(BF16)
    chunk = 256
    parts = [slice(start, start + chunk) for start in range(0, hidden_cols, chunk)]
    low = low_ref[...]
    d_out = d_out_ref[...]

    def ahead(part):
        return nn(low, first_ref[0, :, part]), nt(d_out, second_ref[0, part, :])

    out = None
    back = None
    later = ahead(parts[0])
    for n, part in enumerate(parts):
        pre, d_hidden = later
        if n + 1 < len(parts):
            later = ahead(parts[n + 1])
        act, slope = gelu_pair(pre)
        act = act.astype(BF16)
        d_pre = (d_hidden * slope).astype(BF16)
        hidden_ref[:, part] = act
        d_pre_ref[:, part] = d_pre
        piece = nn(act, second_ref[0, part, :])
        out = piece if out is None else out + piece
        piece = nt(d_pre, first_ref[0, :, part])
        back = piece if back is None else back + piece
    given = out.astype(BF16)
    out_ref[0] = given
    d_gate = jnp.sum(given.astype(F32) * grad_ref[0].astype(F32), axis=1, keepdims=True)
    high = d_gate.astype(BF16).astype(F32)
    wide = jnp.where(lane == 0, high, jnp.where(lane == 1, d_gate - high, 0.0))
    extra = rows_of(wide, rows)
    back = back.astype(BF16)
    for r in range(count):

        @pl.when(step == r)
        def _():
            back_refs[r][:rows] = back
            back_refs[r][rows:] = extra


def expert_apply(at, sources, lane, received, grad, weights, router_w, experts, stride, kept):
    pick, first, second = weights
    groups, rows, _ = grad.shape
    wide = first[0].shape[2]
    total = groups * rows
    count = len(received)

    def flat(width):
        return pl.BlockSpec((rows, width), lambda j, *_: (at + j, 0))

    kept_shapes = (
        jax.ShapeDtypeStruct((groups, rows, D), BF16),
        jax.ShapeDtypeStruct((total, wide), BF16),
        jax.ShapeDtypeStruct((total, wide), BF16),
        jax.ShapeDtypeStruct((total, D), BF16),
        jax.ShapeDtypeStruct((total, D), BF16),
    )
    source = pl.BlockSpec((1, rows, D), lambda j, sources, *_: (sources[j], 0, 0))
    anywhere = pl.BlockSpec(memory_space=pl.ANY)
    given = count + 5 + 2 * len(first)
    results = pl.pallas_call(
        partial(expert_kernel, experts, count, len(first)),
        out_shape=(jax.ShapeDtypeStruct((stride, D), BF16),) * count + kept_shapes,
        grid_spec=pltpu.PrefetchScalarGridSpec(
            num_scalar_prefetch=3,
            in_specs=[whole((rows, D))] * count
            + [source, whole((D, LANES))]
            + [anywhere] * (2 * len(first) + len(kept)),
            out_specs=(whole((stride, D)),) * count
            + (source, flat(wide), flat(wide), flat(D), flat(D)),
            grid=(count,),
            scratch_shapes=[
                pltpu.VMEM((1, D, wide), BF16),
                pltpu.VMEM((1, wide, D), BF16),
                pltpu.SemaphoreType.DMA((2,)),
            ],
        ),
        input_output_aliases={given + n: count + n for n in range(len(kept))},
        compiler_params=params(),
        name="expert_apply",
        cost_estimate=pl.CostEstimate(
            flops=15 * count * rows * D * wide,
            bytes_accessed=count * rows * wide * 4,
            transcendentals=0,
        ),
    )(sources, lane, pick, *received, grad, router_w, *first, *second, *kept)
    return results[:count], results[count:]


def expert_grads_kernel(core_ref, low_ref, d_out_ref, hidden_ref, d_pre_ref, keep_ref, give_ref):
    first = tn(low_ref[...], d_pre_ref[...]).astype(BF16)
    second = tn(hidden_ref[...], d_out_ref[...]).astype(BF16)
    even = core_ref[0] == 0

    @pl.when(even)
    def _():
        keep_ref[0] = first
        give_ref[0] = second

    @pl.when(jnp.logical_not(even))
    def _():
        keep_ref[0] = second
        give_ref[0] = first


def expert_grads(core, low, d_out, hidden, d_pre):
    total, wide = hidden.shape
    block = pl.BlockSpec((1, D, D), lambda i: (i, 0, 0))
    return pl.pallas_call(
        expert_grads_kernel,
        out_shape=(jax.ShapeDtypeStruct((wide // D, D, D), BF16),) * 2,
        in_specs=[
            pl.BlockSpec(memory_space=pltpu.SMEM),
            whole((total, D)),
            whole((total, D)),
            pl.BlockSpec((total, D), lambda i: (0, i)),
            pl.BlockSpec((total, D), lambda i: (0, i)),
        ],
        out_specs=(block, block),
        grid=(wide // D,),
        compiler_params=params(),
        name="expert_grads",
        cost_estimate=pl.CostEstimate(
            flops=8 * total * D * wide, bytes_accessed=total * wide * 4, transcendentals=0
        ),
    )(core, low, d_out, hidden, d_pre)


def pair_kernel(picks_ref, keep_ref, got_ref, *out_refs):
    step = pl.program_id(0)
    total = (keep_ref[0].astype(F32) + got_ref[0].astype(F32)).astype(BF16)
    for r, out_ref in enumerate(out_refs):

        @pl.when(step == r)
        def _():
            out_ref[...] = total


def pair_quarters(picks, keep, got):
    quarter = pl.BlockSpec((1, D, D), lambda i, picks: (picks[i], 0, 0))
    return pl.pallas_call(
        pair_kernel,
        out_shape=(jax.ShapeDtypeStruct((D, D), BF16),) * 4,
        grid_spec=pltpu.PrefetchScalarGridSpec(
            num_scalar_prefetch=1,
            in_specs=[quarter, quarter],
            out_specs=(pl.BlockSpec((D, D), lambda i, picks: (0, 0)),) * 4,
            grid=(4,),
        ),
        compiler_params=params(),
        name="pair_quarters",
        cost_estimate=pl.CostEstimate(flops=D * D, bytes_accessed=D * D * 24, transcendentals=0),
    )(picks, keep, got)


def join_kernel(turn_ref, a_ref, b_ref, c_ref, d_ref, own_a_ref, own_c_ref, out_ref):
    def total(one_ref, two_ref, own_ref, flag):
        own = jnp.where(flag != 0, own_ref[...].astype(F32), 0.0)
        return (one_ref[...].astype(F32) + two_ref[...].astype(F32) + own).astype(BF16)

    left = total(a_ref, b_ref, own_a_ref, turn_ref[1])
    right = total(c_ref, d_ref, own_c_ref, turn_ref[2])
    straight = turn_ref[0] == 0

    @pl.when(straight)
    def _():
        out_ref[0] = left
        out_ref[1] = right

    @pl.when(jnp.logical_not(straight))
    def _():
        out_ref[0] = right
        out_ref[1] = left


def join_quarters(turn, pieces):
    return pl.pallas_call(
        join_kernel,
        out_shape=jax.ShapeDtypeStruct((2, D, D), BF16),
        in_specs=[pl.BlockSpec(memory_space=pltpu.SMEM)] + [whole((D, D))] * 6,
        out_specs=whole((2, D, D)),
        grid=(1,),
        compiler_params=params(),
        name="join_quarters",
        cost_estimate=pl.CostEstimate(flops=D * D, bytes_accessed=D * D * 12, transcendentals=0),
    )(turn, *pieces)


def unfold_kernel(corner_ref, *refs):
    first_ref, second_ref = refs[-2:]
    step = pl.program_id(0)
    for r in range(4):

        @pl.when(step == r)
        def _():
            first_ref[0] = refs[r][0].astype(F32)
            second_ref[0] = refs[r][1].astype(F32)


def unfold(corner, pieces):
    return pl.pallas_call(
        unfold_kernel,
        out_shape=(
            jax.ShapeDtypeStruct((1, D, 4 * D), F32),
            jax.ShapeDtypeStruct((1, 4 * D, D), F32),
        ),
        grid_spec=pltpu.PrefetchScalarGridSpec(
            num_scalar_prefetch=1,
            in_specs=[pl.BlockSpec((2, D, D), lambda i, corner: (0, 0, 0))] * 4,
            out_specs=(
                pl.BlockSpec((1, D, D), lambda i, corner: (0, 0, i ^ corner[0])),
                pl.BlockSpec((1, D, D), lambda i, corner: (0, i ^ corner[0], 0)),
            ),
            grid=(4,),
        ),
        compiler_params=params(),
        name="unfold",
        cost_estimate=pl.CostEstimate(
            flops=400_000 * D * D, bytes_accessed=D * D * 48, transcendentals=0
        ),
    )(corner, *pieces)


def selector_cols(first, second, slots):
    slot = lax.broadcasted_iota(jnp.int32, (first.shape[0], slots), 1)
    hit = (slot == first) | (slot == second)
    return jnp.where(hit, 1.0, 0.0).astype(BF16)


def backward_kernel(experts, capacity_rows, *refs):
    backward_body(experts, capacity_rows, refs[:experts], *refs[experts:])


def backward_body(
    experts,
    capacity_rows,
    back_refs,
    flat_ref,
    cot_ref,
    resid_ref,
    router_ref,
    low_two_ref,
    mixed_ref,
    packed_ref,
    log_ref,
    x_ref,
    gain_one_ref,
    gain_two_ref,
    router_w_ref,
    out_w_ref,
    order_ref,
    core_ref,
    d_resid_ref,
    d_packed_ref,
    keep_ref,
    give_ref,
    returned_ref,
    gate_ref,
    qkv_grad_ref,
    out_grad_ref,
    router_grad_ref,
    gain_two_grad_ref,
):
    step = pl.program_id(0)
    stride = capacity_rows + EXTRA
    slots = experts * stride

    @pl.when(step == 0)
    def _():
        lane = lax.broadcasted_iota(jnp.int32, (capacity_rows, LANES), 1)
        for e in range(experts):
            base = e * stride
            returned_ref[base : base + stride] = back_refs[e][...]
            column = columns_of(back_refs[e][capacity_rows:, :], capacity_rows)
            high = column.astype(BF16).astype(F32)
            wide = jnp.where(
                lane == e, high, jnp.where(lane == experts + e, column - high, 0.0)
            )
            gate_ref[base : base + capacity_rows] = wide.astype(BF16)
            gate_ref[base + capacity_rows : base + stride] = jnp.zeros((EXTRA, LANES), BF16)
        qkv_grad_ref[...] = jnp.zeros_like(qkv_grad_ref)
        out_grad_ref[...] = jnp.zeros_like(out_grad_ref)
        router_grad_ref[...] = jnp.zeros_like(router_grad_ref)
        gain_two_grad_ref[...] = jnp.zeros_like(gain_two_grad_ref)

    first, second = flat_ref[:, 0:1], flat_ref[:, 1:2]
    chosen = selector_cols(first, second, slots)
    d_two = nn(chosen, returned_ref[...])
    d_router = nn(chosen, gate_ref[...])
    d_router = d_router + pltpu.roll(d_router, LANES - experts, 1)
    router = router_ref[...]
    d_logits = router * (d_router - jnp.sum(router * d_router, axis=1, keepdims=True))
    high, low = halves(d_logits)
    d_two = d_two + nt(high, router_w_ref[...]) + nt(low, router_w_ref[...])
    low_two = low_two_ref[...]
    router_grad_ref[...] += tn(high, low_two) + tn(low, low_two)
    hat_two, inverse_two = standardise(resid_ref[...])
    gain_two_grad_ref[...] += jnp.sum(d_two * hat_two, axis=0, keepdims=True)
    d_resid = cot_ref[...] + standardise_back(hat_two, inverse_two, gain_two_ref[...], d_two)
    d_resid_ref[...] = d_resid
    d_attn = d_resid.astype(BF16)
    out_grad_ref[...] += tn(mixed_ref[...], d_attn)
    d_mixed = nt(d_attn, out_w_ref[...]).astype(BF16)
    scale = HEAD_DIM ** (-0.5)
    images = log_ref.shape[0]
    for image in range(images):
        rows = slice(image * PATCHES, (image + 1) * PATCHES)
        for quad in range(2):
            at = quad * QUAD
            queries = packed_ref[rows, at : at + QUAD] * scale
            queries = queries.astype(BF16)
            keys = packed_ref[rows, D + at : D + at + QUAD]
            values = packed_ref[rows, 2 * D + at : 2 * D + at + QUAD]
            grads = d_mixed[rows, at : at + QUAD]
            scores = nt(head_stack(keys), queries)
            d_probs = nt(head_stack(values), grads)
            keys_t = jnp.transpose(keys)
            lane = lax.broadcasted_iota(jnp.int32, (PATCHES, QUAD), 1) // HEAD_DIM
            d_values = jnp.zeros((PATCHES, QUAD), F32)
            d_keys = jnp.zeros((PATCHES, QUAD), F32)
            parts = []
            for h in range(4):
                own = slice(h * PATCHES, (h + 1) * PATCHES)
                log_row = log_ref[image, quad * 4 + h : quad * 4 + h + 1, :]
                probs = jnp.exp(scores[own] - log_row)
                d_own = d_probs[own]
                inner = jnp.sum(probs * d_own, axis=0, keepdims=True)
                d_scores = (probs * (d_own - inner)).astype(BF16)
                d_values = jnp.where(lane == h, nn(probs.astype(BF16), grads), d_values)
                d_keys = jnp.where(lane == h, nn(d_scores, queries), d_keys)
                parts.append(nn(keys_t[h * HEAD_DIM : (h + 1) * HEAD_DIM], d_scores))
            d_queries = jnp.transpose(jnp.concatenate(parts, axis=0)) * scale
            d_packed_ref[rows, at : at + QUAD] = d_queries.astype(BF16)
            d_packed_ref[rows, D + at : D + at + QUAD] = d_keys.astype(BF16)
            d_packed_ref[rows, 2 * D + at : 2 * D + at + QUAD] = d_values.astype(BF16)
    hat_one, _ = standardise(x_ref[...].astype(F32))
    low_one = (hat_one * gain_one_ref[...]).astype(BF16)
    qkv_grad_ref[...] += tn(low_one, d_packed_ref[...])

    @pl.when(step == pl.num_programs(0) - 1)
    def _():
        count, height, _ = keep_ref.shape
        piece = height - SMALL
        high, low = halves(router_grad_ref[...])
        router_grad = nn(order_ref[...], high) + nn(order_ref[...], low)
        small = jnp.concatenate(
            [router_grad[:experts], jnp.broadcast_to(gain_two_grad_ref[...], (SMALL, D))],
            axis=0,
        ).astype(BF16)

        def spread(low_ref, high_ref):
            for j in range(2 * count):
                target = low_ref if j < count else high_ref
                block, at = divmod(j * piece, D)
                if block < 3:
                    rows = qkv_grad_ref[at : at + piece, block * D : (block + 1) * D]
                else:
                    rows = out_grad_ref[at : at + piece, :]
                target[j % count, :piece] = rows.astype(BF16)
                if j * SMALL < experts + SMALL:
                    target[j % count, piece:] = small[j * SMALL : (j + 1) * SMALL]
                else:
                    target[j % count, piece:] = jnp.zeros((SMALL, D), BF16)

        @pl.when(core_ref[0] == 0)
        def _():
            spread(keep_ref, give_ref)

        @pl.when(core_ref[0] != 0)
        def _():
            spread(give_ref, keep_ref)


def attention_backward(
    returned,
    flat,
    cot,
    resid,
    router,
    low_two,
    mixed,
    packed,
    logs,
    x,
    gain_one,
    gain_two,
    router_w,
    out_w,
    order,
    core,
    experts,
    capacity_rows,
    pieces,
    block,
):
    toks = x.shape[0]
    height = 4 * D // pieces + SMALL
    rows = block * PATCHES
    images = toks // PATCHES
    stride = returned[0].shape[0]
    slots = experts * stride

    def tile(width):
        return pl.BlockSpec((rows, width), lambda i: (i, 0))

    return pl.pallas_call(
        partial(backward_kernel, experts, capacity_rows),
        out_shape=(
            jax.ShapeDtypeStruct((toks, D), F32),
            jax.ShapeDtypeStruct((toks, 3 * D), BF16),
            jax.ShapeDtypeStruct((pieces // 2, height, D), BF16),
            jax.ShapeDtypeStruct((pieces // 2, height, D), BF16),
        ),
        in_specs=[whole((stride, D))] * experts
        + [
            tile(8),
            tile(D),
            tile(D),
            tile(LANES),
            tile(D),
            tile(D),
            tile(3 * D),
            pl.BlockSpec((block, HEADS, PATCHES), lambda i: (i, 0, 0)),
            tile(D),
            whole((1, D)),
            whole((1, D)),
            whole((D, LANES)),
            whole((D, D)),
            whole((LANES, LANES)),
            pl.BlockSpec(memory_space=pltpu.SMEM),
        ],
        out_specs=(
            tile(D),
            tile(3 * D),
            whole((pieces // 2, height, D)),
            whole((pieces // 2, height, D)),
        ),
        grid=(images // block,),
        scratch_shapes=[
            pltpu.VMEM((slots, D), BF16),
            pltpu.VMEM((slots, LANES), BF16),
            pltpu.VMEM((D, 3 * D), F32),
            pltpu.VMEM((D, D), F32),
            pltpu.VMEM((LANES, D), F32),
            pltpu.VMEM((1, D), F32),
        ],
        compiler_params=params(),
        name="attention_backward",
        cost_estimate=pl.CostEstimate(
            flops=70_000_000_000, bytes_accessed=toks * D * 20, transcendentals=0
        ),
    )(
        *returned,
        flat,
        cot,
        resid,
        router,
        low_two,
        mixed,
        packed,
        logs,
        x,
        gain_one,
        gain_two,
        router_w,
        out_w,
        order,
        core,
    )


def input_kernel(d_packed_ref, d_resid_ref, x_ref, gain_one_ref, qkv_ref, grad_ref):
    d_one = nt(d_packed_ref[...], qkv_ref[...])
    hat, inverse = standardise(x_ref[...].astype(F32))
    grad_ref[...] = d_resid_ref[...] + standardise_back(hat, inverse, gain_one_ref[...], d_one)


def input_backward(d_packed, d_resid, x, gain_one, qkv, block):
    toks = x.shape[0]
    rows = block * PATCHES

    def tile(width):
        return pl.BlockSpec((rows, width), lambda i: (i, 0))

    return pl.pallas_call(
        input_kernel,
        out_shape=jax.ShapeDtypeStruct((toks, D), F32),
        in_specs=[tile(3 * D), tile(D), tile(D), whole((1, D)), whole((D, 3 * D))],
        out_specs=tile(D),
        grid=(toks // rows,),
        compiler_params=params(),
        name="input_backward",
        cost_estimate=pl.CostEstimate(
            flops=toks * D, bytes_accessed=toks * D, transcendentals=0
        ),
    )(d_packed, d_resid, x, gain_one, qkv)


def combine_kernel(experts, rows, stride, mine_ref, flat_ref, outputs_ref, resid_ref, router_ref, block_ref):
    first, second = flat_ref[:, 0:1], flat_ref[:, 1:2]
    lane = lax.broadcasted_iota(jnp.int32, router_ref.shape, 1) * stride
    router = router_ref[...]

    def gate(flat):
        mine = (flat >= lane) & (flat < lane + stride)
        return jnp.sum(jnp.where(mine, router, 0.0), axis=1, keepdims=True)

    position = lax.broadcasted_iota(jnp.int32, (1, experts * rows), 1)
    owner = jnp.zeros_like(position)
    for e in range(1, experts):
        owner = owner + (position >= e * rows).astype(jnp.int32)
    slot = (owner ^ mine_ref[0]) * stride + (position - owner * rows)
    weight = jnp.where(slot == first, gate(first), jnp.where(slot == second, gate(second), 0.0))
    block_ref[...] = (resid_ref[...] + nn(weight.astype(BF16), outputs_ref[...])).astype(BF16)


def combine(mine, flat, outputs, resid, router, experts, stride, block):
    slots = outputs.shape[0]
    toks = resid.shape[0]
    rows = block * PATCHES

    def tile(width):
        return pl.BlockSpec((rows, width), lambda i: (i, 0))

    return pl.pallas_call(
        partial(combine_kernel, experts, slots // experts, stride),
        out_shape=jax.ShapeDtypeStruct((toks, D), BF16),
        in_specs=[
            pl.BlockSpec(memory_space=pltpu.SMEM),
            tile(8),
            whole((slots, D)),
            tile(D),
            tile(LANES),
        ],
        out_specs=tile(D),
        grid=(toks // rows,),
        compiler_params=params(),
        name="combine",
        cost_estimate=pl.CostEstimate(
            flops=toks * D, bytes_accessed=toks * D, transcendentals=0
        ),
    )(mine, flat, outputs, resid, router)


def finish_kernel(
    experts,
    core_ref,
    own_ref,
    other_ref,
    gain_one_ref,
    qkv_w_ref,
    qkv_ref,
    out_ref,
    router_ref,
    gain_two_ref,
    gain_one_grad_ref,
):
    count, height, _ = own_ref.shape
    piece = height - SMALL

    def spread(low_ref, high_ref):
        for j in range(2 * count):
            source = low_ref if j < count else high_ref
            rows = source[j % count, :piece].astype(F32)
            block, at = divmod(j * piece, D)
            if block < 3:
                qkv_ref[at : at + piece, block * D : (block + 1) * D] = rows
            else:
                out_ref[at : at + piece, :] = rows
            at = j * SMALL
            if at < experts:
                router_ref[at : at + SMALL] = source[j % count, piece:].astype(F32)
            elif at == experts:
                gain_two_ref[...] = source[j % count, piece : piece + 1].astype(F32)

    @pl.when(core_ref[0] == 0)
    def _():
        spread(own_ref, other_ref)

    @pl.when(core_ref[0] != 0)
    def _():
        spread(other_ref, own_ref)

    column = jnp.sum(qkv_ref[...] * qkv_w_ref[...].astype(F32), axis=1, keepdims=True)
    row = jnp.transpose(jnp.broadcast_to(column, (D, LANES)))[0:1]
    gain_one_grad_ref[...] = row / gain_one_ref[...]


def finish(core, own, other, gain_one, qkv, experts):
    count, height, _ = own.shape
    shapes = ((D, 3 * D), (D, D), (experts, D), (1, D), (1, D))
    return pl.pallas_call(
        partial(finish_kernel, experts),
        out_shape=tuple(jax.ShapeDtypeStruct(shape, F32) for shape in shapes),
        in_specs=[
            pl.BlockSpec(memory_space=pltpu.SMEM),
            whole((count, height, D)),
            whole((count, height, D)),
            whole((1, D)),
            whole((D, 3 * D)),
        ],
        out_specs=tuple(whole(shape) for shape in shapes),
        grid=(1,),
        compiler_params=params(),
        name="finish",
        cost_estimate=pl.CostEstimate(flops=D * D * 8, bytes_accessed=D * D * 24, transcendentals=0),
    )(core, own, other, gain_one, qkv)


SWAP = ((0, 1), (1, 0))


def spread_out(values, axes):
    return lax.all_to_all(values, axes, split_axis=0, concat_axis=0, tiled=True)


def sum_everywhere(keep, give, sums, beside, plan):
    got = lax.ppermute(give, "core", SWAP)
    pair = (keep.astype(F32) + got.astype(F32)).astype(BF16)
    sums = plan.join_grads(sums)
    pair, sums = lax.optimization_barrier((pair, sums))
    sums = plan.share_grads(sums)
    spread = spread_out(pair, plan.chips)
    spread, beside = lax.optimization_barrier((spread, beside))
    total = jnp.sum(spread.astype(F32), axis=0, keepdims=True).astype(BF16)
    total = jnp.broadcast_to(total, pair.shape)
    own = spread_out(total, plan.chips)
    return own, sums, beside


class Straight:
    def __init__(self, mesh):
        dp, expert = mesh.devices.shape
        self.devices = dp * expert
        self.sends = self.works = [range(k, k + 4) for k in range(0, expert, 4)]
        self.mesh = Mesh(mesh.devices.reshape(dp, expert // 2, 2), ("dp", "chip", "core"))
        self.everyone = ("dp", "chip", "core")
        self.owners = ("chip", "core")
        self.chips = ("dp", "chip")

    def mine(self):
        return jnp.zeros((), jnp.int32)

    def lane(self):
        return lax.axis_index(("chip", "core"))

    def place(self, expert):
        return expert

    def exchange(self, values):
        return spread_out(values, ("chip", "core"))

    def scatter(self, pieces):
        moved = self.exchange(jnp.stack(pieces))
        return [moved[k] for k in range(len(pieces))]

    def weights(self, first, second):
        return first, second

    def pass_on(self, weights, after):
        return (jnp.zeros((2,), jnp.int32), [weights[0]], [weights[1]]), after

    def start_grads(self, first, second):
        first = first.transpose(1, 0, 2).reshape(1, D, -1)
        second = second.reshape(1, -1, D)
        return lax.psum(first, "dp"), lax.psum(second, "dp")

    def join_grads(self, sums):
        return sums

    def share_grads(self, sums):
        return sums

    def end_grads(self, sums):
        return sums[0].astype(F32), sums[1].astype(F32)

    def core(self):
        return jnp.zeros((1,), jnp.int32)


class Halves:
    def __init__(self, mesh):
        self.devices = 32
        self.sends = [(1, 2, 4, 0), (7, 3, 5, 6)]
        self.works = [(0, 1, 2, 4), (3, 5, 6, 7)]
        self.mesh = Mesh(mesh.devices.reshape(2, 2, 2, 2, 2), ("y", "x", "zh", "zl", "core"))
        self.everyone = ("y", "x", "zh", "zl", "core")
        self.owners = ("zh", "zl", "core")
        self.chips = ("y", "x", "zh", "zl")
        bits = (0, 1)
        self.all = [(y, x, h, l, c) for y in bits for x in bits for h in bits for l in bits for c in bits]

    def mine(self):
        return lax.axis_index(("y", "x", "zl"))

    def lane(self):
        return jnp.zeros((), jnp.int32)

    def place(self, expert):
        low = (expert >> 1) & 1
        y = ((expert >> 2) & 1) ^ lax.axis_index("zh") ^ low
        return (4 * y + 2 * (expert & 1) + low) ^ self.mine()

    def exchange(self, values):
        return spread_out(values, ("y", "x", "zl"))

    def scatter(self, pieces):
        return [
            lax.ppermute(piece, ("y", "x", "zl"), [(i, i ^ k) for i in range(8)]) if k else piece
            for k, piece in enumerate(pieces)
        ]

    def send(self, values, route):
        pairs = []
        for source in self.all:
            target = route(*source)
            if target is not None and target != source:
                pairs.append((self.all.index(source), self.all.index(target)))
        return lax.ppermute(values, self.everyone, pairs)

    def weights(self, first, second):
        def start(core):
            def route(y, x, h, l, c):
                if c != x:
                    return None
                return (y, x, h, l, 1 - x) if y == l else (y, x, 1 - h, l, core)

            return route

        first_in = self.send(first, start(0))
        second_in = self.send(second, start(1))
        return first, second, first_in, second_in

    def pass_on(self, weights, after):
        def passed(core):
            return lambda y, x, h, l, c: (y, x, h, l, 1 - c) if y != l and c == core else None

        first, second, first_in, second_in = weights
        (first_in, second_in), after = lax.optimization_barrier(((first_in, second_in), after))
        first_on = self.send(first_in, passed(0))
        second_on = self.send(second_in, passed(1))
        y, x, low, core = (lax.axis_index(name) for name in ("y", "x", "zl", "core"))
        near = (core ^ x) & 1
        pick = jnp.stack([jnp.where(y == low, near, 1 + core), jnp.where(y == low, near, 2 - core)])
        return (pick, [first, first_in, first_on], [second, second_in, second_on]), after

    def core(self):
        return lax.axis_index("core").reshape(1)

    def start_grads(self, keep, give):
        y, x, core = (lax.axis_index(name) for name in ("y", "x", "core"))
        got = lax.ppermute(give, "core", SWAP)
        rounds = [(ry, rx) for rx in (0, 1) for ry in (0, 1)]
        picks = jnp.stack([2 * (y ^ ry) + (x ^ rx ^ core) for ry, rx in rounds])
        quarters = pair_quarters(picks, keep, got)
        sent = [
            self.send(quarter, lambda y, x, h, l, c: (y ^ ry, x ^ rx ^ c, h ^ y ^ l, l, x))
            for quarter, (ry, rx) in zip(quarters, rounds)
        ]
        return sent + [quarters[0], quarters[2]]

    def join_grads(self, pieces):
        y, x, low, core = (lax.axis_index(name) for name in ("y", "x", "zl", "core"))
        home = (y == low) & (x == core)
        turn = jnp.stack(
            [x ^ core, (home & (core == 0)).astype(jnp.int32), (home & (core == 1)).astype(jnp.int32)]
        )
        return join_quarters(turn, pieces)

    def share_grads(self, mine):
        return [mine] + [
            lax.ppermute(mine, ("y", "x"), [(i, i ^ step) for i in range(4)]) for step in (1, 2, 3)
        ]

    def end_grads(self, pieces):
        y, x = lax.axis_index("y"), lax.axis_index("x")
        return unfold((2 * y + x).reshape(1), pieces)


def shards(
    plan,
    tokens,
    gain_one,
    w_qkv,
    w_attn_out,
    gain_two,
    w_router,
    w_first,
    w_second,
    expert_ids,
    priority_ranks,
    cotangent,
):
    tok_rows = tokens.shape[0]
    experts = w_router.shape[1]
    capacity = max(2, tok_rows // experts)
    capacity_rows = -(-capacity // 16) * 16
    stride = capacity_rows + EXTRA
    gain_one = gain_one.reshape(1, D)
    gain_two = gain_two.reshape(1, D)
    places = plan.place(jnp.arange(experts, dtype=jnp.int32))
    order = (places[:, None] == jnp.arange(LANES, dtype=jnp.int32)).astype(BF16)
    router_w = jnp.dot(w_router, order, preferred_element_type=F32).astype(BF16)
    order = jnp.pad(order, ((0, LANES - experts), (0, 0)))

    mine = plan.mine().reshape(1)
    lane = plan.lane().reshape(1)

    weights = plan.weights(w_first, w_second)
    flat, flat_cols = route(plan.place(expert_ids.T), priority_ranks, experts, capacity, stride)
    grad_rows = plan.exchange(dispatch_grad(mine, flat, cotangent, experts, capacity_rows, stride))
    packed, logs, mixed, resid, low_two, router = attention_forward(
        tokens, gain_one, w_qkv, w_attn_out, gain_two, router_w, experts, 4
    )
    pieces = [None] * experts
    for steps in plan.sends:
        some = dispatch(flat, low_two, steps, capacity_rows, stride)
        flat, some = lax.optimization_barrier((flat, some))
        for k, piece in zip(steps, some):
            pieces[k] = piece
    weights, pieces[0] = plan.pass_on(weights, pieces[0])
    received = plan.scatter(pieces)
    back = [None] * experts
    kept = ()
    at = 0
    for steps in plan.works:
        sources = jnp.asarray(steps, jnp.int32) ^ mine
        some, kept = expert_apply(
            at,
            sources,
            lane,
            [received[k] for k in steps],
            grad_rows,
            weights,
            router_w,
            experts,
            stride,
            kept,
        )
        at += len(steps)
        for k, piece in zip(steps, some):
            back[k] = piece
    outputs, hidden, d_pre, d_out, low = kept
    returned = plan.scatter(back)
    early = [returned[k] for k in plan.works[0]]
    low, early = lax.optimization_barrier((low, early))
    for k, piece in zip(plan.works[0], early):
        returned[k] = piece
    keep, give = expert_grads(plan.core(), low, d_out, hidden, d_pre)
    returned, keep, give, outputs = lax.optimization_barrier((returned, keep, give, outputs))
    outputs = plan.exchange(outputs)
    sums = plan.start_grads(keep, give)
    core = lax.axis_index("core").reshape(1)
    d_resid, d_packed, keep, give = attention_backward(
        returned,
        flat_cols,
        cotangent,
        resid,
        router,
        low_two,
        mixed,
        packed,
        logs,
        tokens,
        gain_one,
        gain_two,
        router_w,
        w_attn_out,
        order,
        core,
        experts,
        capacity_rows,
        plan.devices,
        4,
    )
    keep, give, d_packed, outputs, sums = lax.optimization_barrier(
        (keep, give, d_packed, outputs, sums)
    )
    grad_tokens = input_backward(d_packed, d_resid, tokens, gain_one, w_qkv, 4)
    outputs = outputs.reshape(experts * capacity_rows, D)
    block_out = combine(mine, flat_cols, outputs, resid, router, experts, stride, 4)
    own, sums, beside = sum_everywhere(keep, give, sums, (grad_tokens, block_out), plan)
    grad_tokens, block_out = beside
    first_grad, second_grad = plan.end_grads(sums)
    own, first_grad, second_grad = lax.optimization_barrier((own, first_grad, second_grad))
    other = lax.ppermute(own, "core", SWAP)
    qkv_grad, out_grad, router_grad, gain_two_grad, gain_one_grad = finish(
        core, own, other, gain_one, w_qkv, experts
    )
    return (
        block_out,
        grad_tokens,
        gain_one_grad.reshape(D),
        qkv_grad,
        out_grad,
        gain_two_grad.reshape(D),
        router_grad.T,
        first_grad,
        second_grad,
    )


def solution(mesh):
    plan = Halves(mesh) if mesh.devices.shape == (4, 8) else Straight(mesh)
    both = P(plan.everyone, None)
    one = P(plan.owners, None, None)
    in_specs = (both, P(), P(), P(), P(), P(), one, one, both, both, both)
    out_specs = (both, both, P(), P(), P(), P(), P(), one, one)
    return jax.shard_map(
        partial(shards, plan),
        mesh=plan.mesh,
        in_specs=in_specs,
        out_specs=out_specs,
        check_vma=False,
    )
```

```python
from functools import partial

import jax
import jax.numpy as jnp
from jax import lax
from jax.experimental import pallas as pl
from jax.experimental.pallas import tpu as pltpu
from jax.sharding import Mesh
from jax.sharding import PartitionSpec as P

D = 512
HEADS = 8
HEAD_DIM = 64
PATCHES = 144
QUAD = 256
EPSILON = 1e-06
EXTRA = 16
SMALL = 8
LANES = 128
F32 = jnp.float32
BF16 = jnp.bfloat16
VMEM_LIMIT = 60 * 1024 * 1024


def nn(a, b):
    return lax.dot_general(a, b, (((1,), (0,)), ((), ())), preferred_element_type=F32)


def nt(a, b):
    return lax.dot_general(a, b, (((1,), (1,)), ((), ())), preferred_element_type=F32)


def tn(a, b):
    return lax.dot_general(a, b, (((0,), (0,)), ((), ())), preferred_element_type=F32)


def standardise(values):
    average = jnp.mean(values, axis=-1, keepdims=True)
    centred = values - average
    variance = jnp.mean(centred * centred, axis=-1, keepdims=True)
    inverse = lax.rsqrt(variance + EPSILON)
    return centred * inverse, inverse


def standardise_back(hat, inverse, gain, grad):
    scaled = grad * gain
    mean_one = jnp.mean(scaled, axis=-1, keepdims=True)
    mean_two = jnp.mean(scaled * hat, axis=-1, keepdims=True)
    return inverse * (scaled - mean_one - hat * mean_two)


def halves(values):
    high = values.astype(BF16)
    low = (values - high.astype(F32)).astype(BF16)
    return high, low


def params(**more):
    return pltpu.CompilerParams(vmem_limit_bytes=VMEM_LIMIT, **more)


def whole(shape):
    zeros = (0,) * len(shape)
    return pl.BlockSpec(shape, lambda *_: zeros)


def route_kernel(experts, capacity, stride, ids_ref, ranks_ref, out_ref, cols_ref):
    toks = ids_ref.shape[1]
    catalog = lax.broadcasted_iota(jnp.int32, (experts, toks), 0)
    first_hot = (ids_ref[0:1, :] == catalog).astype(F32)
    second_hot = (ids_ref[1:2, :] == catalog).astype(F32)
    both = jnp.concatenate([first_hot, second_hot], axis=0).astype(BF16)
    first_total = jnp.sum(first_hot, axis=1, keepdims=True)
    ranks = ranks_ref[...].astype(F32)
    rank_rows = jnp.broadcast_to(ranks, (8, toks))
    rank_cols = jnp.transpose(rank_rows)[:, 0:1]
    tile = 256
    for start in range(0, toks, tile):
        part = slice(start, start + tile)
        earlier = (rank_cols < ranks[:, part]).astype(F32).astype(BF16)
        counted = nn(both, earlier)
        slot_first = jnp.sum(counted[:experts] * first_hot[:, part], axis=0, keepdims=True)
        slot_second = jnp.sum(
            (counted[experts:] + first_total) * second_hot[:, part], axis=0, keepdims=True
        )
        for row, slot in ((0, slot_first), (1, slot_second)):
            slot = slot.astype(jnp.int32)
            flat = ids_ref[row : row + 1, part] * stride + slot
            out_ref[row : row + 1, part] = jnp.where(slot < capacity, flat, -1)
    out_ref[2:, :] = jnp.full((6, toks), -1, jnp.int32)
    cols_ref[...] = jnp.transpose(out_ref[...].astype(F32)).astype(jnp.int32)


def route(ids, ranks, experts, capacity, stride):
    toks = ranks.shape[1]
    return pl.pallas_call(
        partial(route_kernel, experts, capacity, stride),
        out_shape=(
            jax.ShapeDtypeStruct((8, toks), jnp.int32),
            jax.ShapeDtypeStruct((toks, 8), jnp.int32),
        ),
        in_specs=[whole((2, toks)), whole((1, toks))],
        out_specs=(whole((8, toks)), whole((toks, 8))),
        grid=(1,),
        compiler_params=params(),
        name="route",
        cost_estimate=pl.CostEstimate(
            flops=2 * toks * toks * 128, bytes_accessed=toks * 48, transcendentals=0
        ),
    )(ids, ranks)


def selector_rows(base, rows, flat_ref):
    toks = flat_ref.shape[1]
    slot = lax.broadcasted_iota(jnp.int32, (rows, toks), 0) + base
    hit = (slot == flat_ref[0:1, :]) | (slot == flat_ref[1:2, :])
    return jnp.where(hit, 1.0, 0.0).astype(BF16)


def dispatch_grad_kernel(stride, mine_ref, flat_ref, grad_ref, out_ref, low_ref):
    step = pl.program_id(0)

    @pl.when(step == 0)
    def _():
        low_ref[...] = grad_ref[...].astype(BF16)

    count, rows, _ = out_ref.shape

    def ahead(n):
        return selector_rows(((step * count + n) ^ mine_ref[0]) * stride, rows, flat_ref)

    later = ahead(0)
    for n in range(count):
        chosen = later
        if n + 1 < count:
            later = ahead(n + 1)
        out_ref[n] = nn(chosen, low_ref[...]).astype(BF16)


def dispatch_grad(mine, flat, grad, experts, rows, stride):
    toks = grad.shape[0]
    return pl.pallas_call(
        partial(dispatch_grad_kernel, stride),
        out_shape=jax.ShapeDtypeStruct((experts, rows, D), BF16),
        in_specs=[pl.BlockSpec(memory_space=pltpu.SMEM), whole((8, toks)), whole((toks, D))],
        out_specs=pl.BlockSpec((4, rows, D), lambda e: (e, 0, 0)),
        grid=(experts // 4,),
        scratch_shapes=[pltpu.VMEM((toks, D), BF16)],
        compiler_params=params(),
        name="dispatch_grad",
        cost_estimate=pl.CostEstimate(
            flops=4 * toks * experts * rows * D, bytes_accessed=toks * D * 6, transcendentals=0
        ),
    )(mine, flat, grad)


def dispatch_kernel(stride, steps, flat_ref, low_ref, *out_refs):
    rows = out_refs[0].shape[0]
    later = selector_rows(steps[0] * stride, rows, flat_ref)
    for n, out_ref in enumerate(out_refs):
        chosen = later
        if n + 1 < len(steps):
            later = selector_rows(steps[n + 1] * stride, rows, flat_ref)
        out_ref[...] = nn(chosen, low_ref[...]).astype(BF16)


def dispatch(flat, low, steps, rows, stride):
    toks = low.shape[0]
    return pl.pallas_call(
        partial(dispatch_kernel, stride, steps),
        out_shape=(jax.ShapeDtypeStruct((rows, D), BF16),) * len(steps),
        in_specs=[whole((8, toks)), whole((toks, D))],
        out_specs=(whole((rows, D)),) * len(steps),
        grid=(1,),
        compiler_params=params(),
        name="dispatch",
        cost_estimate=pl.CostEstimate(
            flops=4 * toks * len(steps) * rows * D, bytes_accessed=toks * D * 4, transcendentals=0
        ),
    )(flat, low)


def rows_of(wide, rows):
    flipped = jnp.transpose(wide)[:EXTRA]
    return jnp.concatenate([flipped, jnp.zeros((EXTRA, D - rows), F32)], axis=1).astype(BF16)


def columns_of(extra, rows):
    flipped = jnp.transpose(extra.astype(F32))
    return flipped[:rows, 0:1] + flipped[:rows, 1:2]


def router_softmax(low, router_w, experts):
    logits = nn(low, router_w)
    lane = lax.broadcasted_iota(jnp.int32, logits.shape, 1)
    logits = jnp.where(lane < experts, logits, -1e30)
    raised = jnp.exp(logits - jnp.max(logits, axis=1, keepdims=True))
    return raised / jnp.sum(raised, axis=1, keepdims=True)


def head_stack(values):
    lane = lax.broadcasted_iota(jnp.int32, values.shape, 1) // HEAD_DIM
    zero = jnp.zeros_like(values)
    return jnp.concatenate([jnp.where(lane == h, values, zero) for h in range(4)], axis=0)


def forward_kernel(
    experts,
    x_ref,
    gain_one_ref,
    qkv_ref,
    out_w_ref,
    gain_two_ref,
    router_w_ref,
    packed_ref,
    log_ref,
    mixed_ref,
    resid_ref,
    low_two_ref,
    router_ref,
):
    images = log_ref.shape[0]
    x = x_ref[...].astype(F32)
    hat, _ = standardise(x)
    low_one = (hat * gain_one_ref[...]).astype(BF16)
    packed_ref[...] = nn(low_one, qkv_ref[...]).astype(BF16)
    units = [(image, quad) for image in range(images) for quad in range(2)]

    def ahead(image, quad):
        rows = slice(image * PATCHES, (image + 1) * PATCHES)
        at = quad * QUAD
        queries = (packed_ref[rows, at : at + QUAD] * HEAD_DIM ** (-0.5)).astype(BF16)
        keys = packed_ref[rows, D + at : D + at + QUAD]
        values = packed_ref[rows, 2 * D + at : 2 * D + at + QUAD]
        return jnp.transpose(values), nt(head_stack(keys), queries)

    later = ahead(*units[0])
    for n, (image, quad) in enumerate(units):
        values_t, scores = later
        if n + 1 < len(units):
            later = ahead(*units[n + 1])
        parts = []
        for h in range(4):
            own = scores[h * PATCHES : (h + 1) * PATCHES]
            top = jnp.max(own, axis=0, keepdims=True)
            weights = jnp.exp(own - top)
            total = jnp.sum(weights, axis=0, keepdims=True)
            log_ref[image, quad * 4 + h : quad * 4 + h + 1, :] = top + jnp.log(total)
            part = nn(values_t[h * HEAD_DIM : (h + 1) * HEAD_DIM], weights.astype(BF16))
            parts.append(part / total)
        mixed_t = jnp.concatenate(parts, axis=0)
        rows = slice(image * PATCHES, (image + 1) * PATCHES)
        mixed_ref[rows, quad * QUAD : (quad + 1) * QUAD] = jnp.transpose(mixed_t).astype(BF16)
    resid = x + nn(mixed_ref[...], out_w_ref[...])
    resid_ref[...] = resid
    hat_two, _ = standardise(resid)
    low_two = (hat_two * gain_two_ref[...]).astype(BF16)
    low_two_ref[...] = low_two
    router_ref[...] = router_softmax(low_two, router_w_ref[...], experts)


def attention_forward(x, gain_one, qkv, out_w, gain_two, router_w, experts, block):
    toks = x.shape[0]
    rows = block * PATCHES
    images = toks // PATCHES

    def tile(width):
        return pl.BlockSpec((rows, width), lambda i: (i, 0))

    return pl.pallas_call(
        partial(forward_kernel, experts),
        out_shape=(
            jax.ShapeDtypeStruct((toks, 3 * D), BF16),
            jax.ShapeDtypeStruct((images, HEADS, PATCHES), F32),
            jax.ShapeDtypeStruct((toks, D), BF16),
            jax.ShapeDtypeStruct((toks, D), F32),
            jax.ShapeDtypeStruct((toks, D), BF16),
            jax.ShapeDtypeStruct((toks, LANES), F32),
        ),
        in_specs=[
            tile(D),
            whole((1, D)),
            whole((D, 3 * D)),
            whole((D, D)),
            whole((1, D)),
            whole((D, LANES)),
        ],
        out_specs=(
            tile(3 * D),
            pl.BlockSpec((block, HEADS, PATCHES), lambda i: (i, 0, 0)),
            tile(D),
            tile(D),
            tile(D),
            tile(LANES),
        ),
        grid=(images // block,),
        compiler_params=params(),
        name="attention_forward",
        cost_estimate=pl.CostEstimate(
            flops=31_000_000_000, bytes_accessed=toks * D * 20, transcendentals=0
        ),
    )(x, gain_one, qkv, out_w, gain_two, router_w)


GELU_C = 0.7978845608028654
GELU_A = 0.044715


def gelu_pair(v):
    square = v * v
    inner = v * (GELU_C + (GELU_C * GELU_A) * square)
    curve = jnp.tanh(inner)
    half = 0.5 + 0.5 * curve
    slope = half + 0.5 * v * (1.0 - curve * curve) * (GELU_C + (3.0 * GELU_C * GELU_A) * square)
    return v * half, slope


def expert_kernel(experts, count, choices, sources_ref, lane_ref, pick_ref, *refs):
    received_refs = refs[:count]
    grad_ref, router_w_ref = refs[count : count + 2]
    first_choices = refs[count + 2 : count + 2 + choices]
    second_choices = refs[count + 2 + choices : count + 2 + 2 * choices]
    first_ref, second_ref, sem = refs[-3:]
    outs = refs[len(refs) - 3 - count - 5 : -3]
    back_refs = outs[:count]
    out_ref, hidden_ref, d_pre_ref, d_out_ref, low_ref = outs[count:]
    step = pl.program_id(0)

    @pl.when(step == 0)
    def _():
        for at, from_refs, to_ref in ((0, first_choices, first_ref), (1, second_choices, second_ref)):
            for n, from_ref in enumerate(from_refs):

                @pl.when(pick_ref[at] == n)
                def _():
                    pltpu.make_async_copy(from_ref, to_ref, sem.at[at]).start()

        pltpu.make_async_copy(first_choices[0], first_ref, sem.at[0]).wait()
        pltpu.make_async_copy(second_choices[0], second_ref, sem.at[1]).wait()

    rows = low_ref.shape[0]
    hidden_cols = first_ref.shape[2]
    for r in range(count):

        @pl.when(step == r)
        def _():
            low_ref[...] = received_refs[r][...]

    lane = lax.broadcasted_iota(jnp.int32, (rows, LANES), 1)
    router = router_softmax(low_ref[...], router_w_ref[...], experts)
    gate = jnp.sum(jnp.where(lane == lane_ref[0], router, 0.0), axis=1, keepdims=True)
    d_out_ref[...] = (gate * grad_ref[0].astype(F32)).astype(BF16)
    chunk = 256
    parts = [slice(start, start + chunk) for start in range(0, hidden_cols, chunk)]
    low = low_ref[...]
    d_out = d_out_ref[...]

    def ahead(part):
        return nn(low, first_ref[0, :, part]), nt(d_out, second_ref[0, part, :])

    out = None
    back = None
    later = ahead(parts[0])
    for n, part in enumerate(parts):
        pre, d_hidden = later
        if n + 1 < len(parts):
            later = ahead(parts[n + 1])
        act, slope = gelu_pair(pre)
        act = act.astype(BF16)
        d_pre = (d_hidden * slope).astype(BF16)
        hidden_ref[:, part] = act
        d_pre_ref[:, part] = d_pre
        piece = nn(act, second_ref[0, part, :])
        out = piece if out is None else out + piece
        piece = nt(d_pre, first_ref[0, :, part])
        back = piece if back is None else back + piece
    given = out.astype(BF16)
    out_ref[0] = given
    d_gate = jnp.sum(given.astype(F32) * grad_ref[0].astype(F32), axis=1, keepdims=True)
    high = d_gate.astype(BF16).astype(F32)
    wide = jnp.where(lane == 0, high, jnp.where(lane == 1, d_gate - high, 0.0))
    extra = rows_of(wide, rows)
    back = back.astype(BF16)
    for r in range(count):

        @pl.when(step == r)
        def _():
            back_refs[r][:rows] = back
            back_refs[r][rows:] = extra


def expert_apply(at, sources, lane, received, grad, weights, router_w, experts, stride, kept):
    pick, first, second = weights
    groups, rows, _ = grad.shape
    wide = first[0].shape[2]
    total = groups * rows
    count = len(received)

    def flat(width):
        return pl.BlockSpec((rows, width), lambda j, *_: (at + j, 0))

    kept_shapes = (
        jax.ShapeDtypeStruct((groups, rows, D), BF16),
        jax.ShapeDtypeStruct((total, wide), BF16),
        jax.ShapeDtypeStruct((total, wide), BF16),
        jax.ShapeDtypeStruct((total, D), BF16),
        jax.ShapeDtypeStruct((total, D), BF16),
    )
    source = pl.BlockSpec((1, rows, D), lambda j, sources, *_: (sources[j], 0, 0))
    anywhere = pl.BlockSpec(memory_space=pl.ANY)
    given = count + 5 + 2 * len(first)
    results = pl.pallas_call(
        partial(expert_kernel, experts, count, len(first)),
        out_shape=(jax.ShapeDtypeStruct((stride, D), BF16),) * count + kept_shapes,
        grid_spec=pltpu.PrefetchScalarGridSpec(
            num_scalar_prefetch=3,
            in_specs=[whole((rows, D))] * count
            + [source, whole((D, LANES))]
            + [anywhere] * (2 * len(first) + len(kept)),
            out_specs=(whole((stride, D)),) * count
            + (source, flat(wide), flat(wide), flat(D), flat(D)),
            grid=(count,),
            scratch_shapes=[
                pltpu.VMEM((1, D, wide), BF16),
                pltpu.VMEM((1, wide, D), BF16),
                pltpu.SemaphoreType.DMA((2,)),
            ],
        ),
        input_output_aliases={given + n: count + n for n in range(len(kept))},
        compiler_params=params(),
        name="expert_apply",
        cost_estimate=pl.CostEstimate(
            flops=15 * count * rows * D * wide,
            bytes_accessed=count * rows * wide * 4,
            transcendentals=0,
        ),
    )(sources, lane, pick, *received, grad, router_w, *first, *second, *kept)
    return results[:count], results[count:]


def expert_grads_kernel(core_ref, low_ref, d_out_ref, hidden_ref, d_pre_ref, keep_ref, give_ref):
    first = tn(low_ref[...], d_pre_ref[...]).astype(BF16)
    second = tn(hidden_ref[...], d_out_ref[...]).astype(BF16)
    even = core_ref[0] == 0

    @pl.when(even)
    def _():
        keep_ref[0] = first
        give_ref[0] = second

    @pl.when(jnp.logical_not(even))
    def _():
        keep_ref[0] = second
        give_ref[0] = first


def expert_grads(core, low, d_out, hidden, d_pre):
    total, wide = hidden.shape
    block = pl.BlockSpec((1, D, D), lambda i: (i, 0, 0))
    return pl.pallas_call(
        expert_grads_kernel,
        out_shape=(jax.ShapeDtypeStruct((wide // D, D, D), BF16),) * 2,
        in_specs=[
            pl.BlockSpec(memory_space=pltpu.SMEM),
            whole((total, D)),
            whole((total, D)),
            pl.BlockSpec((total, D), lambda i: (0, i)),
            pl.BlockSpec((total, D), lambda i: (0, i)),
        ],
        out_specs=(block, block),
        grid=(wide // D,),
        compiler_params=params(),
        name="expert_grads",
        cost_estimate=pl.CostEstimate(
            flops=8 * total * D * wide, bytes_accessed=total * wide * 4, transcendentals=0
        ),
    )(core, low, d_out, hidden, d_pre)


def pair_kernel(picks_ref, keep_ref, got_ref, *out_refs):
    step = pl.program_id(0)
    total = (keep_ref[0].astype(F32) + got_ref[0].astype(F32)).astype(BF16)
    for r, out_ref in enumerate(out_refs):

        @pl.when(step == r)
        def _():
            out_ref[...] = total


def pair_quarters(picks, keep, got):
    quarter = pl.BlockSpec((1, D, D), lambda i, picks: (picks[i], 0, 0))
    return pl.pallas_call(
        pair_kernel,
        out_shape=(jax.ShapeDtypeStruct((D, D), BF16),) * 4,
        grid_spec=pltpu.PrefetchScalarGridSpec(
            num_scalar_prefetch=1,
            in_specs=[quarter, quarter],
            out_specs=(pl.BlockSpec((D, D), lambda i, picks: (0, 0)),) * 4,
            grid=(4,),
        ),
        compiler_params=params(),
        name="pair_quarters",
        cost_estimate=pl.CostEstimate(flops=D * D, bytes_accessed=D * D * 24, transcendentals=0),
    )(picks, keep, got)


def join_kernel(turn_ref, a_ref, b_ref, c_ref, d_ref, own_a_ref, own_c_ref, out_ref):
    def total(one_ref, two_ref, own_ref, flag):
        own = jnp.where(flag != 0, own_ref[...].astype(F32), 0.0)
        return (one_ref[...].astype(F32) + two_ref[...].astype(F32) + own).astype(BF16)

    left = total(a_ref, b_ref, own_a_ref, turn_ref[1])
    right = total(c_ref, d_ref, own_c_ref, turn_ref[2])
    straight = turn_ref[0] == 0

    @pl.when(straight)
    def _():
        out_ref[0] = left
        out_ref[1] = right

    @pl.when(jnp.logical_not(straight))
    def _():
        out_ref[0] = right
        out_ref[1] = left


def join_quarters(turn, pieces):
    return pl.pallas_call(
        join_kernel,
        out_shape=jax.ShapeDtypeStruct((2, D, D), BF16),
        in_specs=[pl.BlockSpec(memory_space=pltpu.SMEM)] + [whole((D, D))] * 6,
        out_specs=whole((2, D, D)),
        grid=(1,),
        compiler_params=params(),
        name="join_quarters",
        cost_estimate=pl.CostEstimate(flops=D * D, bytes_accessed=D * D * 12, transcendentals=0),
    )(turn, *pieces)


def unfold_kernel(corner_ref, *refs):
    first_ref, second_ref = refs[-2:]
    step = pl.program_id(0)
    for r in range(4):

        @pl.when(step == r)
        def _():
            first_ref[0] = refs[r][0].astype(F32)
            second_ref[0] = refs[r][1].astype(F32)


def unfold(corner, pieces):
    return pl.pallas_call(
        unfold_kernel,
        out_shape=(
            jax.ShapeDtypeStruct((1, D, 4 * D), F32),
            jax.ShapeDtypeStruct((1, 4 * D, D), F32),
        ),
        grid_spec=pltpu.PrefetchScalarGridSpec(
            num_scalar_prefetch=1,
            in_specs=[pl.BlockSpec((2, D, D), lambda i, corner: (0, 0, 0))] * 4,
            out_specs=(
                pl.BlockSpec((1, D, D), lambda i, corner: (0, 0, i ^ corner[0])),
                pl.BlockSpec((1, D, D), lambda i, corner: (0, i ^ corner[0], 0)),
            ),
            grid=(4,),
        ),
        compiler_params=params(),
        name="unfold",
        cost_estimate=pl.CostEstimate(
            flops=400_000 * D * D, bytes_accessed=D * D * 48, transcendentals=0
        ),
    )(corner, *pieces)


def selector_cols(first, second, slots):
    slot = lax.broadcasted_iota(jnp.int32, (first.shape[0], slots), 1)
    hit = (slot == first) | (slot == second)
    return jnp.where(hit, 1.0, 0.0).astype(BF16)


def backward_kernel(experts, capacity_rows, *refs):
    backward_body(experts, capacity_rows, refs[:experts], *refs[experts:])


def backward_body(
    experts,
    capacity_rows,
    back_refs,
    flat_ref,
    cot_ref,
    resid_ref,
    router_ref,
    low_two_ref,
    mixed_ref,
    packed_ref,
    log_ref,
    x_ref,
    gain_one_ref,
    gain_two_ref,
    router_w_ref,
    out_w_ref,
    order_ref,
    core_ref,
    d_resid_ref,
    d_packed_ref,
    keep_ref,
    give_ref,
    returned_ref,
    gate_ref,
    qkv_grad_ref,
    out_grad_ref,
    router_grad_ref,
    gain_two_grad_ref,
):
    step = pl.program_id(0)
    stride = capacity_rows + EXTRA
    slots = experts * stride

    @pl.when(step == 0)
    def _():
        lane = lax.broadcasted_iota(jnp.int32, (capacity_rows, LANES), 1)
        for e in range(experts):
            base = e * stride
            returned_ref[base : base + stride] = back_refs[e][...]
            column = columns_of(back_refs[e][capacity_rows:, :], capacity_rows)
            high = column.astype(BF16).astype(F32)
            wide = jnp.where(
                lane == e, high, jnp.where(lane == experts + e, column - high, 0.0)
            )
            gate_ref[base : base + capacity_rows] = wide.astype(BF16)
            gate_ref[base + capacity_rows : base + stride] = jnp.zeros((EXTRA, LANES), BF16)
        qkv_grad_ref[...] = jnp.zeros_like(qkv_grad_ref)
        out_grad_ref[...] = jnp.zeros_like(out_grad_ref)
        router_grad_ref[...] = jnp.zeros_like(router_grad_ref)
        gain_two_grad_ref[...] = jnp.zeros_like(gain_two_grad_ref)

    first, second = flat_ref[:, 0:1], flat_ref[:, 1:2]
    chosen = selector_cols(first, second, slots)
    d_two = nn(chosen, returned_ref[...])
    d_router = nn(chosen, gate_ref[...])
    d_router = d_router + pltpu.roll(d_router, LANES - experts, 1)
    router = router_ref[...]
    d_logits = router * (d_router - jnp.sum(router * d_router, axis=1, keepdims=True))
    high, low = halves(d_logits)
    d_two = d_two + nt(high, router_w_ref[...]) + nt(low, router_w_ref[...])
    low_two = low_two_ref[...]
    router_grad_ref[...] += tn(high, low_two) + tn(low, low_two)
    hat_two, inverse_two = standardise(resid_ref[...])
    gain_two_grad_ref[...] += jnp.sum(d_two * hat_two, axis=0, keepdims=True)
    d_resid = cot_ref[...] + standardise_back(hat_two, inverse_two, gain_two_ref[...], d_two)
    d_resid_ref[...] = d_resid
    d_attn = d_resid.astype(BF16)
    out_grad_ref[...] += tn(mixed_ref[...], d_attn)
    d_mixed = nt(d_attn, out_w_ref[...]).astype(BF16)
    scale = HEAD_DIM ** (-0.5)
    units = [(image, quad) for image in range(log_ref.shape[0]) for quad in range(2)]
    lane = lax.broadcasted_iota(jnp.int32, (PATCHES, QUAD), 1) // HEAD_DIM

    def ahead(image, quad):
        rows = slice(image * PATCHES, (image + 1) * PATCHES)
        at = quad * QUAD
        queries = (packed_ref[rows, at : at + QUAD] * scale).astype(BF16)
        keys = packed_ref[rows, D + at : D + at + QUAD]
        values = packed_ref[rows, 2 * D + at : 2 * D + at + QUAD]
        grads = d_mixed[rows, at : at + QUAD]
        scores = nt(head_stack(keys), queries)
        d_probs = nt(head_stack(values), grads)
        return queries, jnp.transpose(keys), grads, scores, d_probs

    later = ahead(*units[0])
    for n, (image, quad) in enumerate(units):
        queries, keys_t, grads, scores, d_probs = later
        if n + 1 < len(units):
            later = ahead(*units[n + 1])
        rows = slice(image * PATCHES, (image + 1) * PATCHES)
        at = quad * QUAD
        d_values = jnp.zeros((PATCHES, QUAD), F32)
        d_keys = jnp.zeros((PATCHES, QUAD), F32)
        parts = []
        for h in range(4):
            own = slice(h * PATCHES, (h + 1) * PATCHES)
            log_row = log_ref[image, quad * 4 + h : quad * 4 + h + 1, :]
            probs = jnp.exp(scores[own] - log_row)
            d_own = d_probs[own]
            inner = jnp.sum(probs * d_own, axis=0, keepdims=True)
            d_scores = (probs * (d_own - inner)).astype(BF16)
            d_values = jnp.where(lane == h, nn(probs.astype(BF16), grads), d_values)
            d_keys = jnp.where(lane == h, nn(d_scores, queries), d_keys)
            parts.append(nn(keys_t[h * HEAD_DIM : (h + 1) * HEAD_DIM], d_scores))
        d_queries = jnp.transpose(jnp.concatenate(parts, axis=0)) * scale
        d_packed_ref[rows, at : at + QUAD] = d_queries.astype(BF16)
        d_packed_ref[rows, D + at : D + at + QUAD] = d_keys.astype(BF16)
        d_packed_ref[rows, 2 * D + at : 2 * D + at + QUAD] = d_values.astype(BF16)
    hat_one, _ = standardise(x_ref[...].astype(F32))
    low_one = (hat_one * gain_one_ref[...]).astype(BF16)
    qkv_grad_ref[...] += tn(low_one, d_packed_ref[...])

    @pl.when(step == pl.num_programs(0) - 1)
    def _():
        count, height, _ = keep_ref.shape
        piece = height - SMALL
        high, low = halves(router_grad_ref[...])
        router_grad = nn(order_ref[...], high) + nn(order_ref[...], low)
        small = jnp.concatenate(
            [router_grad[:experts], jnp.broadcast_to(gain_two_grad_ref[...], (SMALL, D))],
            axis=0,
        ).astype(BF16)

        def spread(low_ref, high_ref):
            for j in range(2 * count):
                target = low_ref if j < count else high_ref
                block, at = divmod(j * piece, D)
                if block < 3:
                    rows = qkv_grad_ref[at : at + piece, block * D : (block + 1) * D]
                else:
                    rows = out_grad_ref[at : at + piece, :]
                target[j % count, :piece] = rows.astype(BF16)
                if j * SMALL < experts + SMALL:
                    target[j % count, piece:] = small[j * SMALL : (j + 1) * SMALL]
                else:
                    target[j % count, piece:] = jnp.zeros((SMALL, D), BF16)

        @pl.when(core_ref[0] == 0)
        def _():
            spread(keep_ref, give_ref)

        @pl.when(core_ref[0] != 0)
        def _():
            spread(give_ref, keep_ref)


def attention_backward(
    returned,
    flat,
    cot,
    resid,
    router,
    low_two,
    mixed,
    packed,
    logs,
    x,
    gain_one,
    gain_two,
    router_w,
    out_w,
    order,
    core,
    experts,
    capacity_rows,
    pieces,
    block,
):
    toks = x.shape[0]
    height = 4 * D // pieces + SMALL
    rows = block * PATCHES
    images = toks // PATCHES
    stride = returned[0].shape[0]
    slots = experts * stride

    def tile(width):
        return pl.BlockSpec((rows, width), lambda i: (i, 0))

    return pl.pallas_call(
        partial(backward_kernel, experts, capacity_rows),
        out_shape=(
            jax.ShapeDtypeStruct((toks, D), F32),
            jax.ShapeDtypeStruct((toks, 3 * D), BF16),
            jax.ShapeDtypeStruct((pieces // 2, height, D), BF16),
            jax.ShapeDtypeStruct((pieces // 2, height, D), BF16),
        ),
        in_specs=[whole((stride, D))] * experts
        + [
            tile(8),
            tile(D),
            tile(D),
            tile(LANES),
            tile(D),
            tile(D),
            tile(3 * D),
            pl.BlockSpec((block, HEADS, PATCHES), lambda i: (i, 0, 0)),
            tile(D),
            whole((1, D)),
            whole((1, D)),
            whole((D, LANES)),
            whole((D, D)),
            whole((LANES, LANES)),
            pl.BlockSpec(memory_space=pltpu.SMEM),
        ],
        out_specs=(
            tile(D),
            tile(3 * D),
            whole((pieces // 2, height, D)),
            whole((pieces // 2, height, D)),
        ),
        grid=(images // block,),
        scratch_shapes=[
            pltpu.VMEM((slots, D), BF16),
            pltpu.VMEM((slots, LANES), BF16),
            pltpu.VMEM((D, 3 * D), F32),
            pltpu.VMEM((D, D), F32),
            pltpu.VMEM((LANES, D), F32),
            pltpu.VMEM((1, D), F32),
        ],
        compiler_params=params(),
        name="attention_backward",
        cost_estimate=pl.CostEstimate(
            flops=70_000_000_000, bytes_accessed=toks * D * 20, transcendentals=0
        ),
    )(
        *returned,
        flat,
        cot,
        resid,
        router,
        low_two,
        mixed,
        packed,
        logs,
        x,
        gain_one,
        gain_two,
        router_w,
        out_w,
        order,
        core,
    )


def input_kernel(d_packed_ref, d_resid_ref, x_ref, gain_one_ref, qkv_ref, grad_ref):
    d_one = nt(d_packed_ref[...], qkv_ref[...])
    hat, inverse = standardise(x_ref[...].astype(F32))
    grad_ref[...] = d_resid_ref[...] + standardise_back(hat, inverse, gain_one_ref[...], d_one)


def input_backward(d_packed, d_resid, x, gain_one, qkv, block):
    toks = x.shape[0]
    rows = block * PATCHES

    def tile(width):
        return pl.BlockSpec((rows, width), lambda i: (i, 0))

    return pl.pallas_call(
        input_kernel,
        out_shape=jax.ShapeDtypeStruct((toks, D), F32),
        in_specs=[tile(3 * D), tile(D), tile(D), whole((1, D)), whole((D, 3 * D))],
        out_specs=tile(D),
        grid=(toks // rows,),
        compiler_params=params(),
        name="input_backward",
        cost_estimate=pl.CostEstimate(
            flops=toks * D, bytes_accessed=toks * D, transcendentals=0
        ),
    )(d_packed, d_resid, x, gain_one, qkv)


def combine_kernel(experts, rows, stride, mine_ref, flat_ref, outputs_ref, resid_ref, router_ref, block_ref):
    first, second = flat_ref[:, 0:1], flat_ref[:, 1:2]
    lane = lax.broadcasted_iota(jnp.int32, router_ref.shape, 1) * stride
    router = router_ref[...]

    def gate(flat):
        mine = (flat >= lane) & (flat < lane + stride)
        return jnp.sum(jnp.where(mine, router, 0.0), axis=1, keepdims=True)

    position = lax.broadcasted_iota(jnp.int32, (1, experts * rows), 1)
    owner = jnp.zeros_like(position)
    for e in range(1, experts):
        owner = owner + (position >= e * rows).astype(jnp.int32)
    slot = (owner ^ mine_ref[0]) * stride + (position - owner * rows)
    weight = jnp.where(slot == first, gate(first), jnp.where(slot == second, gate(second), 0.0))
    block_ref[...] = (resid_ref[...] + nn(weight.astype(BF16), outputs_ref[...])).astype(BF16)


def combine(mine, flat, outputs, resid, router, experts, stride, block):
    slots = outputs.shape[0]
    toks = resid.shape[0]
    rows = block * PATCHES

    def tile(width):
        return pl.BlockSpec((rows, width), lambda i: (i, 0))

    return pl.pallas_call(
        partial(combine_kernel, experts, slots // experts, stride),
        out_shape=jax.ShapeDtypeStruct((toks, D), BF16),
        in_specs=[
            pl.BlockSpec(memory_space=pltpu.SMEM),
            tile(8),
            whole((slots, D)),
            tile(D),
            tile(LANES),
        ],
        out_specs=tile(D),
        grid=(toks // rows,),
        compiler_params=params(),
        name="combine",
        cost_estimate=pl.CostEstimate(
            flops=toks * D, bytes_accessed=toks * D, transcendentals=0
        ),
    )(mine, flat, outputs, resid, router)


def finish_kernel(
    experts,
    core_ref,
    own_ref,
    other_ref,
    gain_one_ref,
    qkv_w_ref,
    qkv_ref,
    out_ref,
    router_ref,
    gain_two_ref,
    gain_one_grad_ref,
):
    count, height, _ = own_ref.shape
    piece = height - SMALL

    def spread(low_ref, high_ref):
        for j in range(2 * count):
            source = low_ref if j < count else high_ref
            rows = source[j % count, :piece].astype(F32)
            block, at = divmod(j * piece, D)
            if block < 3:
                qkv_ref[at : at + piece, block * D : (block + 1) * D] = rows
            else:
                out_ref[at : at + piece, :] = rows
            at = j * SMALL
            if at < experts:
                router_ref[at : at + SMALL] = source[j % count, piece:].astype(F32)
            elif at == experts:
                gain_two_ref[...] = source[j % count, piece : piece + 1].astype(F32)

    @pl.when(core_ref[0] == 0)
    def _():
        spread(own_ref, other_ref)

    @pl.when(core_ref[0] != 0)
    def _():
        spread(other_ref, own_ref)

    column = jnp.sum(qkv_ref[...] * qkv_w_ref[...].astype(F32), axis=1, keepdims=True)
    row = jnp.transpose(jnp.broadcast_to(column, (D, LANES)))[0:1]
    gain_one_grad_ref[...] = row / gain_one_ref[...]


def finish(core, own, other, gain_one, qkv, experts):
    count, height, _ = own.shape
    shapes = ((D, 3 * D), (D, D), (experts, D), (1, D), (1, D))
    return pl.pallas_call(
        partial(finish_kernel, experts),
        out_shape=tuple(jax.ShapeDtypeStruct(shape, F32) for shape in shapes),
        in_specs=[
            pl.BlockSpec(memory_space=pltpu.SMEM),
            whole((count, height, D)),
            whole((count, height, D)),
            whole((1, D)),
            whole((D, 3 * D)),
        ],
        out_specs=tuple(whole(shape) for shape in shapes),
        grid=(1,),
        compiler_params=params(),
        name="finish",
        cost_estimate=pl.CostEstimate(flops=D * D * 8, bytes_accessed=D * D * 24, transcendentals=0),
    )(core, own, other, gain_one, qkv)


SWAP = ((0, 1), (1, 0))


def spread_out(values, axes):
    return lax.all_to_all(values, axes, split_axis=0, concat_axis=0, tiled=True)


def sum_everywhere(keep, give, sums, beside, plan):
    got = lax.ppermute(give, "core", SWAP)
    pair = (keep.astype(F32) + got.astype(F32)).astype(BF16)
    sums = plan.join_grads(sums)
    pair, sums = lax.optimization_barrier((pair, sums))
    sums = plan.share_grads(sums)
    spread = spread_out(pair, plan.chips)
    spread, beside = lax.optimization_barrier((spread, beside))
    total = jnp.sum(spread.astype(F32), axis=0, keepdims=True).astype(BF16)
    total = jnp.broadcast_to(total, pair.shape)
    own = spread_out(total, plan.chips)
    return own, sums, beside


class Straight:
    def __init__(self, mesh):
        dp, expert = mesh.devices.shape
        self.devices = dp * expert
        self.sends = self.works = [range(k, k + 4) for k in range(0, expert, 4)]
        self.mesh = Mesh(mesh.devices.reshape(dp, expert // 2, 2), ("dp", "chip", "core"))
        self.everyone = ("dp", "chip", "core")
        self.owners = ("chip", "core")
        self.chips = ("dp", "chip")

    def mine(self):
        return jnp.zeros((), jnp.int32)

    def lane(self):
        return lax.axis_index(("chip", "core"))

    def place(self, expert):
        return expert

    def exchange(self, values):
        return spread_out(values, ("chip", "core"))

    def scatter(self, pieces):
        moved = self.exchange(jnp.stack(pieces))
        return [moved[k] for k in range(len(pieces))]

    def weights(self, first, second):
        return first, second

    def pass_on(self, weights, after):
        return (jnp.zeros((2,), jnp.int32), [weights[0]], [weights[1]]), after

    def start_grads(self, first, second):
        first = first.transpose(1, 0, 2).reshape(1, D, -1)
        second = second.reshape(1, -1, D)
        return lax.psum(first, "dp"), lax.psum(second, "dp")

    def join_grads(self, sums):
        return sums

    def share_grads(self, sums):
        return sums

    def end_grads(self, sums):
        return sums[0].astype(F32), sums[1].astype(F32)

    def core(self):
        return jnp.zeros((1,), jnp.int32)


class Halves:
    def __init__(self, mesh):
        self.devices = 32
        self.sends = [(1, 2, 4, 0), (7, 3, 5, 6)]
        self.works = [(0, 1, 2, 4), (3, 5, 6, 7)]
        self.mesh = Mesh(mesh.devices.reshape(2, 2, 2, 2, 2), ("y", "x", "zh", "zl", "core"))
        self.everyone = ("y", "x", "zh", "zl", "core")
        self.owners = ("zh", "zl", "core")
        self.chips = ("y", "x", "zh", "zl")
        bits = (0, 1)
        self.all = [(y, x, h, l, c) for y in bits for x in bits for h in bits for l in bits for c in bits]

    def mine(self):
        return lax.axis_index(("y", "x", "zl"))

    def lane(self):
        return jnp.zeros((), jnp.int32)

    def place(self, expert):
        low = (expert >> 1) & 1
        y = ((expert >> 2) & 1) ^ lax.axis_index("zh") ^ low
        return (4 * y + 2 * (expert & 1) + low) ^ self.mine()

    def exchange(self, values):
        return spread_out(values, ("y", "x", "zl"))

    def scatter(self, pieces):
        return [
            lax.ppermute(piece, ("y", "x", "zl"), [(i, i ^ k) for i in range(8)]) if k else piece
            for k, piece in enumerate(pieces)
        ]

    def send(self, values, route):
        pairs = []
        for source in self.all:
            target = route(*source)
            if target is not None and target != source:
                pairs.append((self.all.index(source), self.all.index(target)))
        return lax.ppermute(values, self.everyone, pairs)

    def weights(self, first, second):
        def start(core):
            def route(y, x, h, l, c):
                if c != x:
                    return None
                return (y, x, h, l, 1 - x) if y == l else (y, x, 1 - h, l, core)

            return route

        first_in = self.send(first, start(0))
        second_in = self.send(second, start(1))
        return first, second, first_in, second_in

    def pass_on(self, weights, after):
        def passed(core):
            return lambda y, x, h, l, c: (y, x, h, l, 1 - c) if y != l and c == core else None

        first, second, first_in, second_in = weights
        (first_in, second_in), after = lax.optimization_barrier(((first_in, second_in), after))
        first_on = self.send(first_in, passed(0))
        second_on = self.send(second_in, passed(1))
        y, x, low, core = (lax.axis_index(name) for name in ("y", "x", "zl", "core"))
        near = (core ^ x) & 1
        pick = jnp.stack([jnp.where(y == low, near, 1 + core), jnp.where(y == low, near, 2 - core)])
        return (pick, [first, first_in, first_on], [second, second_in, second_on]), after

    def core(self):
        return lax.axis_index("core").reshape(1)

    def start_grads(self, keep, give):
        y, x, core = (lax.axis_index(name) for name in ("y", "x", "core"))
        got = lax.ppermute(give, "core", SWAP)
        rounds = [(ry, rx) for rx in (0, 1) for ry in (0, 1)]
        picks = jnp.stack([2 * (y ^ ry) + (x ^ rx ^ core) for ry, rx in rounds])
        quarters = pair_quarters(picks, keep, got)
        sent = [
            self.send(quarter, lambda y, x, h, l, c: (y ^ ry, x ^ rx ^ c, h ^ y ^ l, l, x))
            for quarter, (ry, rx) in zip(quarters, rounds)
        ]
        return sent + [quarters[0], quarters[2]]

    def join_grads(self, pieces):
        y, x, low, core = (lax.axis_index(name) for name in ("y", "x", "zl", "core"))
        home = (y == low) & (x == core)
        turn = jnp.stack(
            [x ^ core, (home & (core == 0)).astype(jnp.int32), (home & (core == 1)).astype(jnp.int32)]
        )
        return join_quarters(turn, pieces)

    def share_grads(self, mine):
        return [mine] + [
            lax.ppermute(mine, ("y", "x"), [(i, i ^ step) for i in range(4)]) for step in (1, 2, 3)
        ]

    def end_grads(self, pieces):
        y, x = lax.axis_index("y"), lax.axis_index("x")
        return unfold((2 * y + x).reshape(1), pieces)


def shards(
    plan,
    tokens,
    gain_one,
    w_qkv,
    w_attn_out,
    gain_two,
    w_router,
    w_first,
    w_second,
    expert_ids,
    priority_ranks,
    cotangent,
):
    tok_rows = tokens.shape[0]
    experts = w_router.shape[1]
    capacity = max(2, tok_rows // experts)
    capacity_rows = -(-capacity // 16) * 16
    stride = capacity_rows + EXTRA
    gain_one = gain_one.reshape(1, D)
    gain_two = gain_two.reshape(1, D)
    places = plan.place(jnp.arange(experts, dtype=jnp.int32))
    order = (places[:, None] == jnp.arange(LANES, dtype=jnp.int32)).astype(BF16)
    router_w = jnp.dot(w_router, order, preferred_element_type=F32).astype(BF16)
    order = jnp.pad(order, ((0, LANES - experts), (0, 0)))

    mine = plan.mine().reshape(1)
    lane = plan.lane().reshape(1)

    weights = plan.weights(w_first, w_second)
    flat, flat_cols = route(plan.place(expert_ids.T), priority_ranks, experts, capacity, stride)
    grad_rows = plan.exchange(dispatch_grad(mine, flat, cotangent, experts, capacity_rows, stride))
    packed, logs, mixed, resid, low_two, router = attention_forward(
        tokens, gain_one, w_qkv, w_attn_out, gain_two, router_w, experts, 4
    )
    pieces = [None] * experts
    for steps in plan.sends:
        some = dispatch(flat, low_two, steps, capacity_rows, stride)
        flat, some = lax.optimization_barrier((flat, some))
        for k, piece in zip(steps, some):
            pieces[k] = piece
    weights, pieces[0] = plan.pass_on(weights, pieces[0])
    received = plan.scatter(pieces)
    back = [None] * experts
    kept = ()
    at = 0
    for steps in plan.works:
        sources = jnp.asarray(steps, jnp.int32) ^ mine
        some, kept = expert_apply(
            at,
            sources,
            lane,
            [received[k] for k in steps],
            grad_rows,
            weights,
            router_w,
            experts,
            stride,
            kept,
        )
        at += len(steps)
        for k, piece in zip(steps, some):
            back[k] = piece
    outputs, hidden, d_pre, d_out, low = kept
    returned = plan.scatter(back)
    early = [returned[k] for k in plan.works[0]]
    low, early = lax.optimization_barrier((low, early))
    for k, piece in zip(plan.works[0], early):
        returned[k] = piece
    keep, give = expert_grads(plan.core(), low, d_out, hidden, d_pre)
    returned, keep, give, outputs = lax.optimization_barrier((returned, keep, give, outputs))
    outputs = plan.exchange(outputs)
    sums = plan.start_grads(keep, give)
    core = lax.axis_index("core").reshape(1)
    d_resid, d_packed, keep, give = attention_backward(
        returned,
        flat_cols,
        cotangent,
        resid,
        router,
        low_two,
        mixed,
        packed,
        logs,
        tokens,
        gain_one,
        gain_two,
        router_w,
        w_attn_out,
        order,
        core,
        experts,
        capacity_rows,
        plan.devices,
        4,
    )
    keep, give, d_packed, outputs, sums = lax.optimization_barrier(
        (keep, give, d_packed, outputs, sums)
    )
    grad_tokens = input_backward(d_packed, d_resid, tokens, gain_one, w_qkv, 4)
    outputs = outputs.reshape(experts * capacity_rows, D)
    block_out = combine(mine, flat_cols, outputs, resid, router, experts, stride, 4)
    own, sums, beside = sum_everywhere(keep, give, sums, (grad_tokens, block_out), plan)
    grad_tokens, block_out = beside
    first_grad, second_grad = plan.end_grads(sums)
    own, first_grad, second_grad = lax.optimization_barrier((own, first_grad, second_grad))
    other = lax.ppermute(own, "core", SWAP)
    qkv_grad, out_grad, router_grad, gain_two_grad, gain_one_grad = finish(
        core, own, other, gain_one, w_qkv, experts
    )
    return (
        block_out,
        grad_tokens,
        gain_one_grad.reshape(D),
        qkv_grad,
        out_grad,
        gain_two_grad.reshape(D),
        router_grad.T,
        first_grad,
        second_grad,
    )


def solution(mesh):
    plan = Halves(mesh) if mesh.devices.shape == (4, 8) else Straight(mesh)
    both = P(plan.everyone, None)
    one = P(plan.owners, None, None)
    in_specs = (both, P(), P(), P(), P(), P(), one, one, both, both, both)
    out_specs = (both, both, P(), P(), P(), P(), P(), one, one)
    return jax.shard_map(
        partial(shards, plan),
        mesh=plan.mesh,
        in_specs=in_specs,
        out_specs=out_specs,
        check_vma=False,
    )
```
